512 devices in a mesh: var: 16 (over y, core), seq: 32 (over x, z).
Axes of the slice: x: 4, y: 8, z: 8, core: 2. Of those that a mesh axis runs over, the one named last changes fastest.
Arguments:
- tokens: bfloat16 [48, 2048, 4096], P('var', 'seq'), may hold values from -6 to 6
- agg_query: bfloat16 [32, 4096], replicated, may hold values from -2.109375 to 2.109375
- agg_value: bfloat16 [4096, 4096], P('var', 'seq'), may hold values from -0.09375 to 0.09375
- w_query: bfloat16 [4096, 4096], P('var', 'seq'), may hold values from -0.09375 to 0.09375
- w_key: bfloat16 [4096, 4096], P('var', 'seq'), may hold values from -0.09375 to 0.09375
- w_value: bfloat16 [4096, 4096], P('var', 'seq'), may hold values from -0.09375 to 0.09375
- gain: float32 [4096], replicated, may hold values from 0.25 to 1.75
- d_out: bfloat16 [32, 64, 4096], P(None, 'var', 'seq'), may hold values from -6 to 6
Outputs:
- attended: bfloat16 [32, 64, 4096], P(None, 'var', 'seq')
- d_tokens: bfloat16 [48, 2048, 4096], P('var', 'seq')
- d_query: float32 [32, 4096], replicated
The draws below stay inside these ranges and needn't reach their ends.
All inputs are finite; a program needn't handle non-finite values.
Results may differ from the reference program's by a relative error of at most 0.035.
Values may be sent and summed in bfloat16 or wider, within the bound.
A program may use at most 64 MiB of HBM per device.

```python
import jax
import jax.numpy as jnp
from jax import lax

D = 4096
H = 32
HD = 128
PATCH_DEV = 64
VARS = 48
PATCHES = 2048
N_SEQ = 32


def block_levels(own_key, extent, pieces, least, high):
    level, own = 1.0, jax.random.fold_in(own_key, 6)
    for axis_at, parts in pieces:
        steps = jnp.exp(jax.random.uniform(jax.random.fold_in(own, axis_at), (parts,), jnp.float32, least / len(pieces), high / len(pieces)))
        level = level * jnp.repeat(steps, extent[axis_at] // parts).reshape([-1 if axis == axis_at else 1 for axis in range(len(extent))])
    return level


def bell_draw(rng, dims, deviation, most, shards=(), kind=jnp.bfloat16):
    drawn = jax.random.normal(rng, dims, jnp.float32) * deviation
    if len(shards) > 0:
        drawn = block_levels(rng, dims, shards, -0.22, 0.18) * drawn
    return jnp.clip(drawn, min=-most, max=most).astype(kind)


def setup_inputs(seed: int = 0) -> dict:
    key_list = jax.random.split(jax.random.key(seed), 9)
    return {
        "tokens": bell_draw(key_list[0], (VARS, PATCHES, D), 1.0, 6.0, ((0, 16), (1, 32))),
        "agg_query": bell_draw(key_list[1], (H, D), (2.0 * (HD / D) ** 0.5), 2.109375),
        "agg_value": bell_draw(key_list[2], (D, D), D ** -0.5, 0.09375, ((0, 16), (1, 32))),
        "w_query": bell_draw(key_list[3], (D, D), D ** -0.5, 0.09375, ((0, 16), (1, 32))),
        "w_key": bell_draw(key_list[4], (D, D), D ** -0.5, 0.09375, ((0, 16), (1, 32))),
        "w_value": bell_draw(key_list[5], (D, D), D ** -0.5, 0.09375, ((0, 16), (1, 32))),
        "gain": jnp.clip(1.0 + 0.15 * jax.random.normal(key_list[6], (D,), jnp.float32), 0.25, 1.75),
        "d_out": bell_draw(key_list[7], (N_SEQ, PATCH_DEV, D), 1.0, 6.0, ((1, 16), (2, 32))),
    }


EPS = 1e-05

def rounded(values):
    return lax.optimization_barrier(values.astype(jnp.bfloat16)).astype(jnp.float32)

def reference(tokens, agg_query, agg_value, w_query, w_key, w_value, gain, d_out):
    factor = HD ** (-0.5)
    query_f = agg_query.astype(jnp.float32)
    blocks = PATCHES // PATCH_DEV

    def mixing(block_id):
        tok_blk = lax.dynamic_slice_in_dim(tokens, block_id * PATCH_DEV, PATCH_DEV, 1).astype(jnp.float32)
        scores = jnp.einsum('vpd,hd->vph', tok_blk, query_f) * factor
        mixw = jax.nn.softmax(scores, axis=0)
        return (tok_blk, mixw, rounded(mixw))

    def forward_block(block_id):
        tok_blk, mixw, mix_b = mixing(block_id)
        return jnp.einsum('vph,vpd->phd', mix_b, tok_blk).astype(jnp.bfloat16)
    summary = lax.map(forward_block, jnp.arange(blocks, dtype=jnp.int32)).reshape(PATCHES, H, D)

    def head_value(head_id):
        part = lax.dynamic_index_in_dim(summary, head_id, 1, keepdims=False)
        cols = lax.dynamic_slice_in_dim(agg_value, head_id * HD, HD, 1)
        return jnp.dot(part, cols, preferred_element_type=jnp.float32)
    pooled = lax.map(head_value, jnp.arange(H, dtype=jnp.int32))
    pooled = pooled.transpose(1, 0, 2).reshape(PATCHES, D).astype(jnp.bfloat16)
    pooled_f = pooled.astype(jnp.float32)
    center = lax.optimization_barrier(jnp.mean(pooled_f, axis=1, keepdims=True))
    spread = lax.optimization_barrier(jnp.mean((pooled_f - center) ** 2, axis=1, keepdims=True))
    inv_std = lax.rsqrt(spread + EPS)
    unit = (pooled_f - center) * inv_std
    normed = (unit * gain).astype(jnp.bfloat16)
    queries = jnp.dot(normed, w_query, preferred_element_type=jnp.float32).astype(jnp.bfloat16)
    keys = jnp.dot(normed, w_key, preferred_element_type=jnp.float32).astype(jnp.bfloat16)
    values = jnp.dot(normed, w_value, preferred_element_type=jnp.float32).astype(jnp.bfloat16)
    grad_out = d_out.reshape(PATCHES, D)

    def head_attention(head_id):

        def cut(mat):
            return lax.dynamic_slice_in_dim(mat, head_id * HD, HD, 1)
        q_h, k_h, v_h, g_h = (cut(queries), cut(keys), cut(values), cut(grad_out))
        logits = jnp.dot(q_h, k_h.T, preferred_element_type=jnp.float32) * factor
        top = lax.optimization_barrier(jnp.max(logits, axis=1, keepdims=True))
        expo = jnp.exp(logits - top)
        probs = expo / lax.optimization_barrier(jnp.sum(expo, axis=1, keepdims=True))
        probs_b = probs.astype(jnp.bfloat16)
        output = jnp.dot(probs_b, v_h, preferred_element_type=jnp.float32).astype(jnp.bfloat16)
        dprob = jnp.dot(g_h, v_h.T, preferred_element_type=jnp.float32)
        inner = lax.optimization_barrier(jnp.sum(probs * dprob, axis=1, keepdims=True))
        dlogit = (probs * (dprob - inner) * factor).astype(jnp.bfloat16)
        dquery = jnp.dot(dlogit, k_h, preferred_element_type=jnp.float32).astype(jnp.bfloat16)
        dkey = jnp.dot(dlogit.T, q_h, preferred_element_type=jnp.float32).astype(jnp.bfloat16)
        dval = jnp.dot(probs_b.T, g_h, preferred_element_type=jnp.float32).astype(jnp.bfloat16)
        return (output, dquery, dkey, dval)
    stacked = lax.map(head_attention, jnp.arange(H, dtype=jnp.int32))
    output, dquery, dkey, dval = [item.transpose(1, 0, 2).reshape(PATCHES, D) for item in stacked]
    attended = output.reshape(N_SEQ, PATCH_DEV, D)
    grad_normed = jnp.dot(dquery, w_query.T, preferred_element_type=jnp.float32)
    grad_normed = grad_normed + jnp.dot(dkey, w_key.T, preferred_element_type=jnp.float32)
    grad_normed = grad_normed + jnp.dot(dval, w_value.T, preferred_element_type=jnp.float32)
    scaled = grad_normed * gain
    d_pooled = inv_std * (scaled - lax.optimization_barrier(jnp.mean(scaled, axis=1, keepdims=True)) - unit * lax.optimization_barrier(jnp.mean(scaled * unit, axis=1, keepdims=True)))
    d_pooled = d_pooled.astype(jnp.bfloat16)

    def head_back(head_id):
        part = lax.dynamic_slice_in_dim(d_pooled, head_id * HD, HD, 1)
        cols = lax.dynamic_slice_in_dim(agg_value, head_id * HD, HD, 1)
        return jnp.dot(part, cols.T, preferred_element_type=jnp.float32).astype(jnp.bfloat16)
    d_summary = lax.map(head_back, jnp.arange(H, dtype=jnp.int32)).transpose(1, 0, 2)

    def backward_block(total, block_id):
        tok_blk, mixw, mix_b = mixing(block_id)
        grad_blk = lax.dynamic_slice_in_dim(d_summary, block_id * PATCH_DEV, PATCH_DEV, 0).astype(jnp.float32)
        dmix = jnp.einsum('vpd,phd->vph', tok_blk, grad_blk)
        dscore = rounded(mixw * (dmix - lax.optimization_barrier(jnp.sum(mixw * dmix, axis=0, keepdims=True))) * factor)
        grad_tok = jnp.einsum('vph,phd->vpd', mix_b, grad_blk) + jnp.einsum('vph,hd->vpd', dscore, query_f)
        total = total + jnp.einsum('vph,vpd->hd', dscore, tok_blk)
        return (total, grad_tok.astype(jnp.bfloat16))
    d_query, grad_blocks = lax.scan(backward_block, jnp.zeros((H, D), jnp.float32), jnp.arange(blocks, dtype=jnp.int32))
    d_tokens = grad_blocks.transpose(1, 0, 2, 3).reshape(VARS, PATCHES, D)
    return (attended, d_tokens, d_query)
```

```python
import functools

import jax
import jax.numpy as jnp
from jax import lax
from jax.experimental import pallas as pl
from jax.experimental.pallas import tpu as pltpu
from jax.sharding import PartitionSpec as P

HD = 128
EPS = 1e-05
NZ = 8
MESH = pl.DeviceIdType.MESH
F32 = jnp.float32
BF16 = jnp.bfloat16


def remote(src, dst, send, recv, device):
    return pltpu.make_async_remote_copy(
        src_ref=src, dst_ref=dst, send_sem=send, recv_sem=recv, device_id=device, device_id_type=MESH
    )


def loop(first, last, body):
    def step(k, carry):
        body(k)
        return carry

    lax.fori_loop(first, last, step, 0)


def slot(ref, j):
    return ref.at[j]


def whole(ref, j):
    return ref


class Direct:
    def __init__(self, axis, n, src=slot, dst=slot):
        self.axis, self.n, self.src, self.dst = axis, n, src, dst

    def sems(self):
        return [pltpu.SemaphoreType.DMA((self.n,)), pltpu.SemaphoreType.DMA((self.n,)), pltpu.SemaphoreType.DMA(())]

    def peers(self):
        me = lax.axis_index(self.axis)
        return [(self.n - 1, lambda k: {self.axis: lax.rem(me + k + 1, self.n)})]

    def kinds(self):
        return [self.axis]

    def own(self, x, o, sems):
        me = lax.axis_index(self.axis)
        return pltpu.make_async_copy(self.src(x, me), self.dst(o, me), sems[2])

    def start(self, x, o, sems):
        me = lax.axis_index(self.axis)

        def send(k):
            to = lax.rem(me + k, self.n)
            remote(self.src(x, to), self.dst(o, me), sems[0].at[k], sems[1].at[k], {self.axis: to}).start()

        loop(1, self.n, send)
        self.own(x, o, sems).start()

    def middle(self, x, o, sems):
        pass

    def finish(self, x, o, sems):
        me = lax.axis_index(self.axis)
        self.own(x, o, sems).wait()

        def wait(k):
            to, source = lax.rem(me + k, self.n), lax.rem(me + self.n - k, self.n)
            remote(self.src(x, to), self.dst(o, source), sems[0].at[k], sems[1].at[k], {self.axis: to}).wait()

        loop(1, self.n, wait)


class GatherSeq:
    def __init__(self, n):
        self.nz = NZ
        self.nx = n // NZ

    def sems(self):
        dma = pltpu.SemaphoreType.DMA
        return [dma((self.nz,)), dma((self.nz,)), dma((self.nz, self.nx)), dma((self.nz, self.nx)), dma(())]

    def place(self):
        me = lax.axis_index("seq")
        return me, me // self.nz, lax.rem(me, self.nz)

    def peers(self):
        me, x, z = self.place()
        return [
            (self.nz - 1, lambda k: {"seq": x * self.nz + lax.rem(z + k + 1, self.nz)}),
            (self.nx - 1, lambda k: {"seq": lax.rem(x + k + 1, self.nx) * self.nz + z}),
        ]

    def kinds(self):
        return ["z", "x"]

    def along_z(self, a, o, sems, k, received):
        me, x, z = self.place()
        at = lax.rem(z + self.nz - k, self.nz) if received else z
        return remote(
            a, o.at[x * self.nz + at], sems[0].at[k], sems[1].at[k],
            {"seq": x * self.nz + lax.rem(z + k, self.nz)},
        )

    def along_x(self, o, sems, k, m, received):
        me, x, z = self.place()
        zz = lax.rem(z + self.nz - k, self.nz)
        src = o.at[x * self.nz + zz]
        row = lax.rem(x + self.nx - m, self.nx) if received else x
        return remote(
            src, o.at[row * self.nz + zz], sems[2].at[k, m], sems[3].at[k, m],
            {"seq": lax.rem(x + m, self.nx) * self.nz + z},
        )

    def start(self, a, o, sems):
        me, x, z = self.place()
        pltpu.make_async_copy(a, o.at[me], sems[4]).start()
        loop(1, self.nz, lambda k: self.along_z(a, o, sems, k, False).start())

    def middle(self, a, o, sems):
        me, x, z = self.place()
        pltpu.make_async_copy(a, o.at[me], sems[4]).wait()
        loop(1, self.nx, lambda m: self.along_x(o, sems, 0, m, False).start())

        def forward(k):
            self.along_z(a, o, sems, k, True).wait_recv()
            loop(1, self.nx, lambda m: self.along_x(o, sems, k, m, False).start())

        loop(1, self.nz, forward)

    def finish(self, a, o, sems):
        loop(1, self.nz, lambda k: self.along_z(a, o, sems, k, False).wait_send())

        def wait(k):
            loop(1, self.nx, lambda m: self.along_x(o, sems, k, m, True).wait())

        loop(0, self.nz, wait)


class GatherVar:
    def __init__(self, n, dst=slot, ring=False):
        self.n, self.ny, self.dst, self.ring = n, n // 2, dst, ring
        self.right = self.ny // 2
        self.left = (self.ny - 1) // 2

    def sems(self):
        dma = pltpu.SemaphoreType.DMA
        return [dma((self.ny,)), dma((self.ny,)), dma((self.ny,)), dma((self.ny,)), dma(())]

    def place(self):
        me = lax.axis_index("var")
        return me, me // 2, lax.rem(me, 2)

    def peers(self):
        me, y, c = self.place()
        across = (1, lambda k: {"var": 2 * y + 1 - c})
        if self.ring:
            near = [(1, lambda k: {"var": 2 * lax.rem(y + 1, self.ny) + c})]
            if self.ny > 2:
                near.append((1, lambda k: {"var": 2 * lax.rem(y + self.ny - 1, self.ny) + c}))
            return near + [across]
        return [(self.ny - 1, lambda k: {"var": 2 * lax.rem(y + k + 1, self.ny) + c}), across]

    def kinds(self):
        return (["y1", "y-1", "core"] if self.ny > 2 else ["y1", "core"]) if self.ring else ["y", "core"]

    def along_y(self, a, o, sems, k, received):
        me, y, c = self.place()
        at = 2 * lax.rem(y + self.ny - k, self.ny) + c if received else me
        return remote(
            a, self.dst(o, at), sems[0].at[k], sems[1].at[k], {"var": 2 * lax.rem(y + k, self.ny) + c}
        )

    def hop(self, a, o, sems, t, way, received):
        me, y, c = self.place()
        k = t if way == 1 else self.ny - t
        behind = t - 1 if not received else t
        at = 2 * lax.rem(y + self.ny * 2 - way * behind, self.ny) + c
        src = a if (isinstance(t, int) and t == 1 and not received) else self.dst(o, at)
        return remote(
            src, self.dst(o, at), sems[0].at[k], sems[1].at[k], {"var": 2 * lax.rem(y + self.ny + way, self.ny) + c}
        )

    def across(self, o, sems, k, received, first=None):
        me, y, c = self.place()
        side = 1 - c if received else c
        at = 2 * lax.rem(y + self.ny - k, self.ny) + side
        src = self.dst(o, at) if first is None else first
        return remote(src, self.dst(o, at), sems[2].at[k], sems[3].at[k], {"var": 2 * y + 1 - c})

    def own(self, a, o, sems):
        return pltpu.make_async_copy(a, self.dst(o, lax.axis_index("var")), sems[4])

    def start(self, a, o, sems):
        if self.ring:
            self.hop(a, o, sems, 1, 1, False).start()
            if self.left:
                self.hop(a, o, sems, 1, -1, False).start()
        else:
            loop(1, self.ny, lambda k: self.along_y(a, o, sems, k, False).start())
        self.across(o, sems, 0, False, a).start()
        self.own(a, o, sems).start()

    def middle(self, a, o, sems):
        if self.ring:
            for t in range(1, self.right + 1):
                self.hop(a, o, sems, t, 1, True).wait_recv()
                if t < self.right:
                    self.hop(a, o, sems, t + 1, 1, False).start()
                self.across(o, sems, t, False).start()
                if t <= self.left:
                    self.hop(a, o, sems, t, -1, True).wait_recv()
                    if t < self.left:
                        self.hop(a, o, sems, t + 1, -1, False).start()
                    self.across(o, sems, self.ny - t, False).start()
        else:
            def forward(k):
                self.along_y(a, o, sems, k, True).wait_recv()
                self.across(o, sems, k, False).start()

            loop(1, self.ny, forward)

    def finish(self, a, o, sems):
        self.own(a, o, sems).wait()
        if self.ring:
            for t in range(1, self.right + 1):
                self.hop(a, o, sems, t, 1, False).wait_send()
                if t <= self.left:
                    self.hop(a, o, sems, t, -1, False).wait_send()
        else:
            loop(1, self.ny, lambda k: self.along_y(a, o, sems, k, False).wait_send())
        self.across(o, sems, 0, False, a).wait_send()
        self.across(o, sems, 0, True).wait_recv()

        def wait(k):
            self.across(o, sems, k, False).wait_send()
            self.across(o, sems, k, True).wait_recv()

        loop(1, self.ny, wait)


def barrier(jobs):
    groups = {}
    for job in jobs:
        for kind, group in zip(job.kinds(), job.peers()):
            groups[kind] = group
    if "seq" in groups:
        groups.pop("z", None), groups.pop("x", None)
    if "var" in groups:
        for kind in ("y", "y1", "y-1", "core"):
            groups.pop(kind, None)
    if "y" in groups:
        groups.pop("y1", None), groups.pop("y-1", None)
    sem = pltpu.get_barrier_semaphore()
    total = 0
    for count, to in groups.values():
        def greet(k, to=to):
            pl.semaphore_signal(sem, inc=1, device_id=to(k), device_id_type=MESH)

        loop(0, count, greet)
        total += count
    pl.semaphore_wait(sem, total)


def exchange(name, cid, jobs, arrays, outs):
    n = len(jobs)
    counts = [len(job.sems()) for job in jobs]

    def kernel(*refs):
        xs, os, rest = refs[:n], refs[n : 2 * n], list(refs[2 * n :])
        sems = []
        for count in counts:
            sems.append(rest[:count])
            rest = rest[count:]
        barrier(jobs)
        for phase in ("start", "middle", "finish"):
            for job, x, o, s in zip(jobs, xs, os, sems):
                getattr(job, phase)(x, o, s)

    return pl.pallas_call(
        kernel,
        name=name,
        out_shape=[jax.ShapeDtypeStruct(*out) for out in outs],
        in_specs=[pl.BlockSpec(memory_space=pl.ANY)] * n,
        out_specs=[pl.BlockSpec(memory_space=pl.ANY)] * n,
        scratch_shapes=[sem for job in jobs for sem in job.sems()],
        compiler_params=pltpu.CompilerParams(collective_id=cid, has_side_effects=True),
    )(*arrays)


def sum_seq(q_ref, z_held, x_held, done, sems, nx, nz):
    me = lax.axis_index("seq")
    x, z = me // nz, lax.rem(me, nz)

    def swap(src, held, place, n, device, sem):
        own = pltpu.make_async_copy(src, held.at[place], sem[2])
        own.start()

        def copy(k, received):
            at = lax.rem(place + n - k, n) if received else place
            return remote(src, held.at[at], sem[0].at[k], sem[1].at[k], device(lax.rem(place + k, n)))

        loop(1, n, lambda k: copy(k, False).start())
        own.wait()
        loop(1, n, lambda k: copy(k, True).wait())
        total = held[0]
        for at in range(1, n):
            total = total + held[at]
        done[...] = total

    swap(q_ref, z_held, z, nz, lambda k: {"seq": x * nz + k}, sems[:3])
    swap(done, x_held, x, nx, lambda k: {"seq": k * nz + z}, sems[3:])


def tokens_back(cid, d_tok, q_part, n_var, n_seq):
    nz, nx = NZ, n_seq // NZ
    _, per, rows, cols = d_tok.shape
    back = Direct("var", n_var, slot, lambda o, j: o.at[:, :, pl.ds(pl.multiple_of(j * cols, cols), cols)])
    spread = GatherVar(n_var, lambda o, j: o.at[:, pl.ds(pl.multiple_of(j * cols, cols), cols)])
    dma = pltpu.SemaphoreType.DMA

    def kernel(t_ref, q_ref, dt_ref, dq_ref, z_held, x_held, done, *sems):
        me = lax.axis_index("seq")
        x, z = me // nz, lax.rem(me, nz)

        barrier([back, GatherSeq(n_seq)])
        back_sems, spread_sems, sum_sems = sems[:3], sems[3:8], sems[8:]
        back.start(t_ref, dt_ref, back_sems)
        sum_seq(q_ref, z_held, x_held, done, sum_sems, nx, nz)
        spread.start(done, dq_ref, spread_sems)
        spread.middle(done, dq_ref, spread_sems)
        spread.finish(done, dq_ref, spread_sems)
        back.finish(t_ref, dt_ref, back_sems)

    heads = q_part.shape[0]
    return pl.pallas_call(
        kernel,
        name="tokens_back",
        out_shape=[
            jax.ShapeDtypeStruct((per, rows, cols * n_var), BF16),
            jax.ShapeDtypeStruct((heads, cols * n_var), F32),
        ],
        in_specs=[pl.BlockSpec(memory_space=pl.ANY)] * 2,
        out_specs=[pl.BlockSpec(memory_space=pl.ANY)] * 2,
        scratch_shapes=[
            pltpu.VMEM((nz, heads, cols), F32),
            pltpu.VMEM((nx, heads, cols), F32),
            pltpu.VMEM((heads, cols), F32),
            *back.sems(),
            *spread.sems(),
            dma((nz,)), dma((nz,)), dma(()), dma((nx,)), dma((nx,)), dma(()),
        ],
        compiler_params=pltpu.CompilerParams(collective_id=cid, has_side_effects=True),
    )(d_tok, q_part)


def per_device(n_var, n_seq, tokens, agg_query, agg_value, w_query, w_key, w_value, gain, d_out):
    factor = HD ** (-0.5)
    per, rows, width = tokens.shape
    heads = agg_query.shape[0]
    n_vars = per * n_var
    cut = width // n_var
    own = rows // n_var
    line = own * heads
    i = lax.axis_index("var")

    local_scores = jnp.einsum("vpd,hd->vph", tokens, agg_query, preferred_element_type=F32) * factor
    flat = per * rows * heads // 128
    grouped, scores, value = exchange(
        "tokens_out",
        0,
        [
            Direct("var", n_var, lambda x, j: x.at[:, :, pl.ds(pl.multiple_of(j * cut, cut), cut)], slot),
            GatherVar(n_var),
            GatherSeq(n_seq),
        ],
        [tokens, local_scores.reshape(flat, 128), agg_value],
        [
            ((n_var, per, rows, cut), BF16),
            ((n_var, flat, 128), F32),
            ((n_seq, cut, HD), BF16),
        ],
    )
    grouped = grouped.reshape(n_vars, rows, cut)
    mixw = jax.nn.softmax(scores.reshape(n_vars, rows, heads), axis=0)
    mix_b = mixw.astype(BF16)
    summary = jnp.einsum("vph,vpd->phd", mix_b, grouped, preferred_element_type=F32).astype(BF16)
    pooled_part = jnp.einsum("phd,hde->phe", summary, value, preferred_element_type=F32).astype(BF16)
    (pooled_in,) = exchange(
        "pooled_sum",
        1,
        [Direct("var", n_var)],
        [pooled_part.reshape(n_var, line, HD)],
        [((n_var, line, HD), BF16)],
    )
    pooled = jnp.sum(pooled_in.astype(F32), axis=0).astype(BF16).astype(F32).reshape(own, heads, HD)
    gain3 = gain.reshape(1, heads, HD)
    center = jnp.mean(pooled, axis=(1, 2), keepdims=True)
    spread = jnp.mean((pooled - center) ** 2, axis=(1, 2), keepdims=True)
    inv_std = lax.rsqrt(spread + EPS)
    unit = (pooled - center) * inv_std
    normed = (unit * gain3).astype(BF16)
    weights = jnp.concatenate([w_query, w_key, w_value], axis=1)
    normed_all, weights_all = exchange(
        "normed_out",
        2,
        [GatherSeq(n_seq), GatherVar(n_var, ring=True)],
        [normed.reshape(line, HD), weights],
        [((n_seq, line, HD), BF16), ((n_var, cut, 3 * HD), BF16)],
    )
    weights_all = weights_all.reshape(width, 3 * HD)
    row_count = n_seq * own
    normed_rows = normed_all.reshape(row_count, width)
    qkv = jnp.dot(normed_rows, weights_all, preferred_element_type=F32).astype(BF16)
    queries = qkv[:, :HD]
    (kv,) = exchange(
        "keys_values",
        3,
        [GatherVar(n_var)],
        [qkv[:, HD:]],
        [((n_var, row_count, 2 * HD), BF16)],
    )
    kv = kv.reshape(n_var * row_count, 2 * HD)
    all_keys, all_values = kv[:, :HD], kv[:, HD:]
    grad_out = d_out.reshape(row_count, HD)
    logits = jnp.einsum("qe,ke->qk", queries, all_keys, preferred_element_type=F32) * factor
    top = jnp.max(logits, axis=1, keepdims=True)
    expo = jnp.exp(logits - top)
    probs = expo / jnp.sum(expo, axis=1, keepdims=True)
    probs_b = probs.astype(BF16)
    attended = jnp.dot(probs_b, all_values, preferred_element_type=F32).astype(BF16)
    dprob = jnp.einsum("qe,ke->qk", grad_out, all_values, preferred_element_type=F32)
    inner = jnp.sum(probs * dprob, axis=1, keepdims=True)
    dlogit = (probs * (dprob - inner) * factor).astype(BF16)
    dquery = jnp.dot(dlogit, all_keys, preferred_element_type=F32).astype(BF16)
    dkey = jnp.einsum("qk,qe->ke", dlogit, queries, preferred_element_type=F32).astype(BF16)
    dval = jnp.einsum("qk,qe->ke", probs_b, grad_out, preferred_element_type=F32).astype(BF16)
    (dkv_in,) = exchange(
        "keys_values_back",
        4,
        [Direct("var", n_var)],
        [jnp.concatenate([dkey, dval], axis=1).reshape(n_var, row_count, 2 * HD)],
        [((n_var, row_count, 2 * HD), BF16)],
    )
    dkv = jnp.sum(dkv_in.astype(F32), axis=0).astype(BF16)
    dqkv = jnp.concatenate([dquery, dkv], axis=1)
    grad_part = jnp.einsum("rc,dc->rd", dqkv, weights_all, preferred_element_type=F32).astype(BF16)
    (grad_in,) = exchange(
        "normed_back",
        5,
        [Direct("seq", n_seq)],
        [grad_part.reshape(n_seq, line, HD)],
        [((n_seq, line, HD), BF16)],
    )
    grad_normed = jnp.sum(grad_in.astype(F32), axis=0).reshape(own, heads, HD)
    scaled = grad_normed * gain3
    mean_scaled = jnp.mean(scaled, axis=(1, 2), keepdims=True)
    mean_dot = jnp.mean(scaled * unit, axis=(1, 2), keepdims=True)
    d_pooled = (inv_std * (scaled - mean_scaled - unit * mean_dot)).astype(BF16)
    (d_pooled_all,) = exchange(
        "pooled_back",
        6,
        [GatherVar(n_var)],
        [d_pooled.reshape(line, HD)],
        [((n_var, line, HD), BF16)],
    )
    d_pooled_all = d_pooled_all.reshape(rows, heads, HD)
    d_summary = jnp.einsum("phe,hde->phd", d_pooled_all, value, preferred_element_type=F32).astype(BF16)
    dmix_part = jnp.einsum("vpd,phd->pvh", grouped, d_summary, preferred_element_type=F32)
    (dmix_in,) = exchange(
        "dmix_sum",
        7,
        [Direct("var", n_var)],
        [dmix_part.reshape(n_var, flat, 128)],
        [((n_var, flat, 128), F32)],
    )
    dmix = jnp.sum(dmix_in, axis=0).reshape(own, n_vars, heads)
    mix_own = lax.dynamic_slice_in_dim(mixw, i * own, own, 1).transpose(1, 0, 2)
    dscore = (mix_own * (dmix - jnp.sum(mix_own * dmix, axis=1, keepdims=True)) * factor).astype(BF16)
    (dscore_all,) = exchange(
        "dscore_out",
        8,
        [GatherVar(n_var)],
        [dscore.reshape(flat, 128)],
        [((n_var, flat, 128), BF16)],
    )
    dscore_all = dscore_all.reshape(rows, n_vars, heads)
    query_cut = lax.dynamic_slice_in_dim(agg_query, i * cut, cut, 1)
    query_part = jnp.einsum("pvh,vpd->hd", dscore_all, grouped, preferred_element_type=F32)
    grad_tok = jnp.einsum("vph,phd->vpd", mix_b, d_summary, preferred_element_type=F32)
    grad_tok = grad_tok + jnp.einsum("pvh,hd->vpd", dscore_all, query_cut, preferred_element_type=F32)
    d_tokens, d_query = tokens_back(
        9, grad_tok.astype(BF16).reshape(n_var, per, rows, cut), query_part, n_var, n_seq
    )
    return (attended.reshape(d_out.shape), d_tokens, d_query)


def solution(mesh):
    return jax.shard_map(
        functools.partial(per_device, mesh.shape["var"], mesh.shape["seq"]),
        mesh=mesh,
        in_specs=(
            P("var", "seq", None),
            P(),
            P("var", "seq"),
            P("var", "seq"),
            P("var", "seq"),
            P("var", "seq"),
            P(),
            P(None, "var", "seq"),
        ),
        out_specs=(P(None, "var", "seq"), P("var", "seq", None), P()),
        check_vma=False,
    )
```

```python
import functools
from types import SimpleNamespace

import jax
import jax.numpy as jnp
from jax import lax
from jax.experimental import pallas as pl
from jax.experimental.pallas import tpu as pltpu
from jax.sharding import PartitionSpec as P

HD = 128
EPS = 1e-05
NZ = 8
MESH = pl.DeviceIdType.MESH
F32 = jnp.float32
BF16 = jnp.bfloat16
VAR, SEQ = "var", "seq"
NT = ((1,), (1,))
TN = ((0,), (0,))


def remote(src, dst, send, recv, device):
    return pltpu.make_async_remote_copy(
        src_ref=src, dst_ref=dst, send_sem=send, recv_sem=recv, device_id=device, device_id_type=MESH
    )


def loop(first, last, body):
    def step(k, carry):
        body(k)
        return carry

    lax.fori_loop(first, last, step, 0)


def slot(ref, j):
    return ref.at[j]


def dma(*shape):
    return pltpu.SemaphoreType.DMA(shape)


class Direct:
    def __init__(self, axis, n, src=slot, dst=slot):
        self.axis, self.n, self.src, self.dst = axis, n, src, dst

    def sems(self):
        return [dma(self.n), dma(self.n), dma()]

    def peers(self):
        me = lax.axis_index(self.axis)
        return [(self.n - 1, lambda k: {self.axis: lax.rem(me + k + 1, self.n)})]

    def copy(self, x, o, sems, k, received):
        me = lax.axis_index(self.axis)
        to = lax.rem(me + k, self.n)
        at = lax.rem(me + self.n - k, self.n) if received else me
        return remote(self.src(x, to), self.dst(o, at), sems[0].at[k], sems[1].at[k], {self.axis: to})

    def own(self, x, o, sems):
        me = lax.axis_index(self.axis)
        return pltpu.make_async_copy(self.src(x, me), self.dst(o, me), sems[2])

    def start(self, x, o, sems):
        self.far(x, o, sems, 0)
        self.near(x, o, sems, 0)

    def far(self, x, o, sems, near):
        loop(near + 1, self.n - near, lambda k: self.copy(x, o, sems, k, False).start())

    def near(self, x, o, sems, near):
        loop(1, near + 1, lambda k: self.copy(x, o, sems, k, False).start())
        loop(self.n - near, self.n, lambda k: self.copy(x, o, sems, k, False).start())
        self.own(x, o, sems).start()

    def landed(self, x, o, sems):
        self.own(x, o, sems).wait()
        loop(1, self.n, lambda k: self.copy(x, o, sems, k, True).wait_recv())

    def sent(self, x, o, sems):
        loop(1, self.n, lambda k: self.copy(x, o, sems, k, False).wait_send())


class GatherSeq:
    def __init__(self, n):
        self.nz = NZ
        self.nx = n // NZ

    def sems(self):
        return [dma(self.nz), dma(self.nz), dma(self.nz, self.nx), dma(self.nz, self.nx), dma()]

    def place(self):
        me = lax.axis_index(SEQ)
        return me, me // self.nz, lax.rem(me, self.nz)

    def peers(self):
        me, x, z = self.place()
        return [
            (self.nz - 1, lambda k: {SEQ: x * self.nz + lax.rem(z + k + 1, self.nz)}),
            (self.nx - 1, lambda k: {SEQ: lax.rem(x + k + 1, self.nx) * self.nz + z}),
        ]

    def along_z(self, a, o, sems, k, received):
        me, x, z = self.place()
        at = lax.rem(z + self.nz - k, self.nz) if received else z
        return remote(
            a, o.at[x * self.nz + at], sems[0].at[k], sems[1].at[k],
            {SEQ: x * self.nz + lax.rem(z + k, self.nz)},
        )

    def along_x(self, a, o, sems, k, m, received):
        me, x, z = self.place()
        zz = lax.rem(z + self.nz - k, self.nz)
        src = a if isinstance(k, int) and k == 0 else o.at[x * self.nz + zz]
        row = lax.rem(x + self.nx - m, self.nx) if received else x
        return remote(
            src, o.at[row * self.nz + zz], sems[2].at[k, m], sems[3].at[k, m],
            {SEQ: lax.rem(x + m, self.nx) * self.nz + z},
        )

    def own(self, a, o, sems):
        return pltpu.make_async_copy(a, o.at[lax.axis_index(SEQ)], sems[4])

    def start(self, a, o, sems):
        loop(1, self.nz, lambda k: self.along_z(a, o, sems, k, False).start())
        loop(1, self.nx, lambda m: self.along_x(a, o, sems, 0, m, False).start())
        self.own(a, o, sems).start()

    def middle(self, a, o, sems):
        def forward(k):
            self.along_z(a, o, sems, k, True).wait_recv()
            loop(1, self.nx, lambda m: self.along_x(a, o, sems, k, m, False).start())

        loop(1, self.nz, forward)

    def landed(self, a, o, sems):
        self.own(a, o, sems).wait()

        def wait(k):
            loop(1, self.nx, lambda m: self.along_x(a, o, sems, k, m, True).wait_recv())

        loop(0, self.nz, wait)

    def sent(self, a, o, sems):
        loop(1, self.nz, lambda k: self.along_z(a, o, sems, k, False).wait_send())

        def wait(k):
            loop(1, self.nx, lambda m: self.along_x(a, o, sems, k, m, False).wait_send())

        loop(0, self.nz, wait)


class GatherVar:
    def __init__(self, n, dst=slot):
        self.n, self.ny, self.dst = n, n // 2, dst

    def sems(self):
        return [dma(self.ny), dma(self.ny), dma(self.ny), dma(self.ny), dma()]

    def place(self):
        me = lax.axis_index(VAR)
        return me, me // 2, lax.rem(me, 2)

    def far(self, src, o, sems, block, way, k):
        me, y, c = self.place()
        at = 2 * lax.rem(y + self.ny - block, self.ny) + c
        src = self.dst(o, at) if src is None else src
        return remote(
            src, self.dst(o, at), sems[0].at[k], sems[1].at[k], {VAR: 2 * lax.rem(y + way, self.ny) + c}
        )

    def arrived(self, a, o, sems, k):
        me, y, c = self.place()
        at = 2 * lax.rem(y + self.ny - k, self.ny) + c
        remote(a, self.dst(o, at), sems[0].at[k], sems[1].at[k], {VAR: 2 * y + 1 - c}).wait_recv()

    def across(self, o, sems, k, received, first=None):
        me, y, c = self.place()
        side = 1 - c if received else c
        at = 2 * lax.rem(y + self.ny - k, self.ny) + side
        src = self.dst(o, at) if first is None else first
        return remote(src, self.dst(o, at), sems[2].at[k], sems[3].at[k], {VAR: 2 * y + 1 - c})

    def own(self, a, o, sems):
        return pltpu.make_async_copy(a, self.dst(o, lax.axis_index(VAR)), sems[4])

    def begin(self, a, o, sems):
        loop(1, self.ny, lambda k: self.far(a, o, sems, 0, k, k).start())

    def start(self, a, o, sems):
        self.begin(a, o, sems)
        self.across(o, sems, 0, False, a).start()
        self.own(a, o, sems).start()

    def middle(self, a, o, sems):
        def forward(k):
            self.arrived(a, o, sems, k)
            self.across(o, sems, k, False).start()

        loop(1, self.ny, forward)

    def landed(self, a, o, sems):
        self.own(a, o, sems).wait()
        loop(0, self.ny, lambda k: self.across(o, sems, k, True).wait_recv())

    def sent(self, a, o, sems):
        loop(1, self.ny, lambda k: self.far(a, o, sems, 0, k, k).wait_send())
        self.across(o, sems, 0, False, a).wait_send()
        loop(1, self.ny, lambda k: self.across(o, sems, k, False).wait_send())


class RingVar(GatherVar):
    def begin(self, a, o, sems):
        self.far(a, o, sems, 0, 1, 1).start()
        self.far(a, o, sems, 0, self.ny - 1, self.ny - 1).start()

    def step(self, a, o, sems, t):
        half = self.ny // 2
        self.arrived(a, o, sems, t)
        if t < half:
            self.far(None, o, sems, t, 1, t + 1).start()
        self.across(o, sems, t, False).start()
        if t < half:
            self.arrived(a, o, sems, self.ny - t)
            if t < half - 1:
                self.far(None, o, sems, self.ny - t, self.ny - 1, self.ny - t - 1).start()
            self.across(o, sems, self.ny - t, False).start()


class TwoStepVar(GatherVar):
    def begin(self, a, o, sems):
        for k in (2, 6, 1, 7):
            self.far(a, o, sems, 0, k, k).start()

    def opposite(self, o, sems):
        me, y, c = self.place()
        return self.far(None, o, sems, 2 + 4 * c, 2 + 4 * c, 4)

    def middle(self, a, o, sems):
        me, y, c = self.place()
        self.arrived(a, o, sems, 2)
        self.arrived(a, o, sems, 6)
        self.opposite(o, sems).start()
        self.far(None, o, sems, 2, 1, 3).start()
        self.far(None, o, sems, 6, 7, 5).start()
        for k in (2, 6):
            self.across(o, sems, k, False).start()
        for k in (1, 7, 3, 5, 4):
            self.arrived(a, o, sems, k)
            self.across(o, sems, k, False).start()


class ReduceVar:
    def __init__(self, n):
        self.n, self.ny = n, n // 2

    def sems(self):
        return [dma(self.ny) for _ in range(4)]

    def place(self):
        me = lax.axis_index(VAR)
        return me // 2, lax.rem(me, 2)

    def across(self, b, held, sems, k):
        y, c = self.place()
        yy = lax.rem(y + k + 1, self.ny)
        return remote(b.at[2 * yy + 1 - c], held.at[yy], sems[0].at[k], sems[1].at[k], {VAR: 2 * y + 1 - c})

    def along_y(self, summed, landed, sems, k, received):
        y, c = self.place()
        yy = lax.rem(y + k + 1, self.ny)
        at = lax.rem(y + self.ny - k - 1, self.ny) if received else y
        return remote(summed.at[yy], landed.at[at], sems[2].at[k], sems[3].at[k], {VAR: 2 * yy + c})

    def start(self, b, held, summed, landed, sems):
        loop(0, self.ny, lambda k: self.across(b, held, sems, k).start())

    def push(self, b, held, summed, landed, sems):
        y, c = self.place()

        def add(k):
            yy = lax.rem(y + k + 1, self.ny)
            self.across(b, held, sems, k).wait_recv()
            total = b[2 * yy + c].astype(F32) + held[yy].astype(F32)
            summed[yy] = total.astype(summed.dtype)

        def step(k):
            add(k)
            self.along_y(summed, landed, sems, k, False).start()

        loop(0, self.ny - 1, step)
        add(self.ny - 1)

    def landed(self, b, held, summed, landed, sems):
        y, c = self.place()
        total = summed[y].astype(F32)
        for k in range(self.ny - 1):
            self.along_y(summed, landed, sems, k, True).wait_recv()
            total = total + landed[lax.rem(y + self.ny - k - 1, self.ny)].astype(F32)
        return total

    def sent(self, b, held, summed, landed, sems):
        loop(0, self.ny, lambda k: self.across(b, held, sems, k).wait_send())
        loop(0, self.ny - 1, lambda k: self.along_y(summed, landed, sems, k, False).wait_send())


class ReduceSeq:
    def __init__(self, n):
        self.nz, self.nx = NZ, n // NZ

    def sems(self):
        return [dma(self.nz, self.nx), dma(self.nz, self.nx), dma(self.nz), dma(self.nz)]

    def place(self):
        me = lax.axis_index(SEQ)
        return me // self.nz, lax.rem(me, self.nz)

    def along_x(self, b, held, sems, k, m, received):
        x, z = self.place()
        zz = lax.rem(z + k + 1, self.nz)
        to = lax.rem(x + m, self.nx)
        row = lax.rem(x + self.nx - m, self.nx) if received else x
        return remote(
            b.at[to * self.nz + zz], held.at[row * self.nz + zz], sems[0].at[k, m], sems[1].at[k, m],
            {SEQ: to * self.nz + z},
        )

    def along_z(self, summed, landed, sems, k, received):
        x, z = self.place()
        zz = lax.rem(z + k + 1, self.nz)
        at = lax.rem(z + self.nz - k - 1, self.nz) if received else z
        return remote(summed.at[zz], landed.at[at], sems[2].at[k], sems[3].at[k], {SEQ: x * self.nz + zz})

    def start(self, b, held, summed, landed, sems):
        def send(k):
            loop(1, self.nx, lambda m: self.along_x(b, held, sems, k, m, False).start())

        loop(0, self.nz, send)

    def push(self, b, held, summed, landed, sems):
        x, z = self.place()

        def add(k):
            zz = lax.rem(z + k + 1, self.nz)
            total = b[x * self.nz + zz].astype(F32)
            for m in range(1, self.nx):
                self.along_x(b, held, sems, k, m, True).wait_recv()
                total = total + held[lax.rem(x + self.nx - m, self.nx) * self.nz + zz].astype(F32)
            summed[zz] = total.astype(summed.dtype)

        def step(k):
            add(k)
            self.along_z(summed, landed, sems, k, False).start()

        loop(0, self.nz - 1, step)
        add(self.nz - 1)

    def landed(self, b, held, summed, landed, sems):
        x, z = self.place()
        total = summed[z].astype(F32)
        for k in range(self.nz - 1):
            self.along_z(summed, landed, sems, k, True).wait_recv()
            total = total + landed[lax.rem(z + self.nz - k - 1, self.nz)].astype(F32)
        return total

    def sent(self, b, held, summed, landed, sems):
        def wait(k):
            loop(1, self.nx, lambda m: self.along_x(b, held, sems, k, m, False).wait_send())

        loop(0, self.nz, wait)
        loop(0, self.nz - 1, lambda k: self.along_z(summed, landed, sems, k, False).wait_send())


class SumAlong:
    def __init__(self, n, along_z):
        self.n, self.along_z = (NZ if along_z else n // NZ), along_z

    def sems(self):
        return [dma(self.n), dma(self.n)]

    def place(self):
        me = lax.axis_index(SEQ)
        return lax.rem(me, NZ) if self.along_z else me // NZ

    def copy(self, src, held, sems, k, received):
        me = lax.axis_index(SEQ)
        here = self.place()
        at = lax.rem(here + self.n - k, self.n) if received else here
        to = lax.rem(here + k, self.n)
        to = me // NZ * NZ + to if self.along_z else to * NZ + lax.rem(me, NZ)
        return remote(src, held.at[at], sems[0].at[k], sems[1].at[k], {SEQ: to})

    def start(self, src, held, sems):
        loop(1, self.n, lambda k: self.copy(src, held, sems, k, False).start())
        held[self.place()] = src[...]

    def landed(self, src, held, sems):
        loop(1, self.n, lambda k: self.copy(src, held, sems, k, True).wait_recv())
        total = held[0]
        for at in range(1, self.n):
            total = total + held[at]
        return total

    def sent(self, src, held, sems):
        loop(1, self.n, lambda k: self.copy(src, held, sems, k, False).wait_send())


def bound(job, sems, refs):
    def fill(phase):
        return lambda *more: phase(*refs, sems, *more)

    return SimpleNamespace(
        **{name: fill(getattr(job, name)) for name in dir(job) if not name.startswith("_") and name != "n"
           and callable(getattr(job, name))}
    )


def barrier(groups):
    sem = pltpu.get_barrier_semaphore()
    for count, to in groups:
        loop(0, count, lambda k: pl.semaphore_signal(sem, inc=1, device_id=to(k), device_id_type=MESH))
    return lambda: pl.semaphore_wait(sem, sum(count for count, _ in groups))


def dot(a, b, dims=((1,), (0,))):
    return lax.dot_general(a, b, (dims, ((), ())), preferred_element_type=F32)


def over_vars(fold, z):
    out = z[:, :128]
    for at in range(128, z.shape[1], 128):
        out = fold(out, z[:, at : at + 128])
    for shift in (64, 32, 16):
        out = fold(out, pltpu.roll(out, shift, 1))
    return jnp.concatenate([out] * (z.shape[1] // 128), axis=1)


def program(n_var, n_seq, tokens, agg_query, agg_value, w_query, w_key, w_value, gain, grad_out):
    factor = HD ** (-0.5)
    per, rows, width = tokens.shape
    heads = agg_query.shape[0]
    octets = heads // 8
    cut = width // n_var
    own = rows // n_var
    line = own * heads
    groups = rows // 16
    chunk = per * 16
    lanes = n_var * chunk
    tall = 16 * heads
    row_count = n_seq * own
    at_once = 16 // own
    ny, nz, nx = n_var // 2, NZ, n_seq // NZ

    at_cut = lambda j: pl.ds(pl.multiple_of(j * cut, cut), cut)
    weight = lambda w: RingVar(n_var, lambda o, j: o.at[j, :, pl.ds(w * HD, HD)])
    jobs = dict(
        tokens=Direct(VAR, n_var, lambda x, j: x.at[:, :, at_cut(j)], slot),
        scores=GatherVar(n_var),
        value=GatherSeq(n_seq),
        pooled=ReduceVar(n_var),
        normed=GatherSeq(n_seq),
        w_query=weight(0),
        w_key=weight(1),
        w_value=weight(2),
        kv=TwoStepVar(n_var),
        dkv=ReduceVar(n_var),
        grad=ReduceSeq(n_seq),
        d_pooled=GatherVar(n_var),
        dmix=ReduceVar(n_var),
        dscore=GatherVar(n_var),
        back=Direct(VAR, n_var, slot, lambda o, j: o.at[:, :, at_cut(j)]),
        query_z=SumAlong(n_seq, True),
        query_x=SumAlong(n_seq, False),
        query=GatherVar(n_var, lambda o, j: o.at[:, at_cut(j)]),
    )

    block = lambda n, r=line, c=HD, t=BF16: ((n, r, c), t)

    def through(blocks, *rest):
        return block(blocks, *rest), block(ny, *rest), block(ny, *rest), block(ny, *rest)

    pooled, dkv = through(n_var), through(n_var, row_count, 2 * HD)
    dmix = through(n_var, 8, lanes, F32)
    buffers = dict(
        grouped=((n_var, per, rows, cut), BF16),
        s_own=((heads, 256), F32),
        s_all=block(n_var, heads, 256, F32),
        value_all=block(n_seq, cut, HD),
        mix=block(n_var, 8, lanes, F32),
        mix_wide=block(groups, tall, lanes),
        mix_tall=block(groups, lanes, tall),
        summary=block(groups, tall, cut),
        stack=block(groups, tall, HD),
        pooled0=pooled[0], pooled1=pooled[1], pooled2=pooled[2], pooled3=pooled[3],
        unit=((line, HD), F32),
        inv=((line, HD), F32),
        normed_own=((line, HD), BF16),
        normed_all=block(n_seq),
        weights=block(n_var, cut, 3 * HD),
        wide=((row_count, width), BF16),
        kv_own=((row_count, 2 * HD), BF16),
        kv_all=block(n_var, row_count, 2 * HD),
        dkv0=dkv[0], dkv1=dkv[1], dkv2=dkv[2], dkv3=dkv[3],
        grad0=block(n_seq), grad1=block(n_seq), grad2=block(nz), grad3=block(nz),
        dp_own=((line, HD), BF16),
        dp_all=block(n_var),
        d_summary=block(groups, tall, cut),
        dmix0=dmix[0], dmix1=dmix[1], dmix2=dmix[2], dmix3=dmix[3],
        dscore_own=((8, lanes), F32),
        dscore_all=block(n_var, 8, lanes, F32),
        back_b=((n_var, per, rows, cut), BF16),
        query_part=((heads, cut), F32),
        query_line=((heads, cut), F32),
        query_done=((heads, cut), F32),
        query_z=block(nz, heads, cut, F32),
        query_x=block(nx, heads, cut, F32),
    )
    results = dict(
        attended=((row_count, HD), BF16),
        mixed=(tokens.shape, BF16),
        dscore=((heads, per * rows), BF16),
        d_query=((heads, width), F32),
    )
    names = [*results, *buffers]
    job_sems = [job.sems() for job in jobs.values()]

    def kernel(tok, aq, av, wq, wk, wv, gn, go, *rest):
        r = SimpleNamespace(**dict(zip(names, rest)))
        refs = dict(
            tokens=(tok, r.grouped),
            scores=(r.s_own, r.s_all),
            value=(av, r.value_all),
            pooled=(r.pooled0, r.pooled1, r.pooled2, r.pooled3),
            normed=(r.normed_own, r.normed_all),
            w_query=(wq, r.weights),
            w_key=(wk, r.weights),
            w_value=(wv, r.weights),
            kv=(r.kv_own, r.kv_all),
            dkv=(r.dkv0, r.dkv1, r.dkv2, r.dkv3),
            grad=(r.grad0, r.grad1, r.grad2, r.grad3),
            d_pooled=(r.dp_own, r.dp_all),
            dmix=(r.dmix0, r.dmix1, r.dmix2, r.dmix3),
            dscore=(r.dscore_own, r.dscore_all),
            back=(r.back_b, r.mixed),
            query_z=(r.query_part, r.query_z),
            query_x=(r.query_line, r.query_x),
            query=(r.query_done, r.d_query),
        )
        left, ready_jobs = list(rest[len(names) :]), {}
        for (name, job), wanted in zip(jobs.items(), job_sems):
            ready_jobs[name] = bound(job, left[: len(wanted)], refs[name])
            left = left[len(wanted) :]
        j = SimpleNamespace(**ready_jobs)
        ring = (j.w_key, j.w_value, j.w_query)

        def t_group(g):
            return r.grouped[:, :, g * 16 : (g + 1) * 16, :].reshape(lanes, cut)

        i = lax.axis_index(VAR)
        greeted = barrier(jobs["tokens"].peers() + jobs["value"].peers())

        rows_here = [tok[v, g * 16 : (g + 1) * 16, :] for g in range(groups) for v in range(per)]
        local = dot(aq[...], jnp.concatenate(rows_here, axis=0), NT) * factor
        r.s_own[...] = jnp.concatenate([local, jnp.zeros((heads, 256 - per * rows), F32)], axis=1)
        greeted()
        j.scores.start()
        j.value.start()
        j.tokens.start()
        j.scores.middle()
        j.value.middle()

        iota = lambda shape, dim: lax.broadcasted_iota(jnp.int32, shape, dim)
        ones = lambda where: where.astype(F32).astype(BF16)
        wide_mask = lax.rem(iota((16, lanes), 1), 16) == iota((16, lanes), 0)
        tall_mask = lax.rem(iota((lanes, tall), 0), 16) == lax.rem(iota((lanes, tall), 1), 16)
        spread_heads = ones(iota((heads, tall), 1) // 16 == iota((heads, tall), 0))
        at, to = iota((tall, tall), 0), iota((tall, tall), 1)
        to_patches = ones(to == lax.rem(at, heads) * 16 + at // heads)
        to_heads = ones(to == lax.rem(at, 16) * heads + at // 16)

        j.scores.landed()
        for g in range(groups):
            z = jnp.concatenate([r.s_all[n, :, g * chunk : (g + 1) * chunk] for n in range(n_var)], axis=1)
            e = jnp.exp(z - over_vars(jnp.maximum, z))
            mixw = e / over_vars(jnp.add, e)
            for o in range(octets):
                r.mix[g * octets + o] = mixw[o * 8 : (o + 1) * 8]
            mix_b = mixw.astype(BF16)
            full = jnp.broadcast_to(mix_b.astype(F32)[:, None, :], (heads, 16, lanes))
            full = jnp.where(wide_mask[None], full, 0.0)
            r.mix_wide[g] = full.astype(BF16).reshape(tall, lanes)
            r.mix_tall[g] = jnp.where(tall_mask, dot(mix_b, spread_heads, TN), 0.0).astype(BF16)
        j.value.landed()
        j.scores.sent()
        j.value.sent()
        j.tokens.landed()
        for w in ring:
            w.start()

        for g in range(groups):
            r.summary[g] = dot(r.mix_wide[g], t_group(g)).astype(BF16)
        for h in range(heads):
            here = slice(h * 16, (h + 1) * 16)
            part = jnp.concatenate([r.summary[g, here, :] for g in range(groups)], axis=0)
            part = dot(part, r.value_all[h]).astype(BF16)
            for g in range(groups):
                r.stack[g, here, :] = part[g * 16 : (g + 1) * 16]
        for g in range(groups):
            part = dot(to_patches, r.stack[g]).astype(BF16)
            for n in range(at_once):
                r.pooled0[g * at_once + n] = part[n * line : (n + 1) * line]
        j.pooled.start()
        j.pooled.push()
        for w in ring:
            w.step(1)
        pooled = j.pooled.landed().astype(BF16).astype(F32).reshape(own, heads, HD)
        mean = lambda a: jnp.sum(jnp.sum(a, axis=1, keepdims=True), axis=2, keepdims=True) / width
        center = mean(pooled)
        inv_std = lax.rsqrt(mean((pooled - center) ** 2) + EPS)
        unit = (pooled - center) * inv_std
        r.normed_own[...] = (unit * gn[...][None]).astype(BF16).reshape(line, HD)
        j.normed.start()
        r.unit[...] = unit.reshape(line, HD)
        r.inv[...] = jnp.broadcast_to(inv_std, (own, heads, HD)).reshape(line, HD)
        for w in ring:
            w.step(2)
        j.normed.middle()
        for t in range(3, ny // 2 + 1):
            for w in ring:
                w.step(t)
        j.normed.landed()

        def widen(g):
            src = r.normed_all[pl.ds(g * at_once, at_once)].reshape(tall, HD)
            part = dot(to_heads, src).astype(BF16)
            for h in range(heads):
                r.wide[pl.ds(pl.multiple_of(g * 16, 16), 16), h * HD : (h + 1) * HD] = part[h * 16 : (h + 1) * 16]

        loop(0, n_seq // at_once, widen)
        j.w_key.landed()
        j.w_value.landed()
        kv_weights = r.weights[:, :, HD:].reshape(width, 2 * HD)
        r.kv_own[...] = dot(r.wide[...], kv_weights).astype(BF16)
        j.kv.start()
        j.w_query.landed()
        queries = dot(r.wide[...], r.weights[:, :, :HD].reshape(width, HD)).astype(BF16)
        j.kv.middle()
        j.kv.landed()

        keys = r.kv_all[:, :, :HD].reshape(n_var * row_count, HD)
        values = r.kv_all[:, :, HD:].reshape(n_var * row_count, HD)
        grad = go[...]
        logits = dot(queries, keys, NT) * factor
        expo = jnp.exp(logits - jnp.max(logits, axis=1, keepdims=True))
        probs = expo / jnp.sum(expo, axis=1, keepdims=True)
        probs_b = probs.astype(BF16)
        dprob = dot(grad, values, NT)
        dlogit = (probs * (dprob - jnp.sum(probs * dprob, axis=1, keepdims=True)) * factor).astype(BF16)
        r.dkv0[:, :, :HD] = dot(dlogit, queries, TN).astype(BF16).reshape(n_var, row_count, HD)
        r.dkv0[:, :, HD:] = dot(probs_b, grad, TN).astype(BF16).reshape(n_var, row_count, HD)
        j.dkv.start()
        r.attended[...] = dot(probs_b, values).astype(BF16)
        dquery = dot(dlogit, keys).astype(BF16)
        j.dkv.push()
        dkv = j.dkv.landed().astype(BF16)

        dqkv = jnp.concatenate([dquery, dkv], axis=1)
        r.wide[...] = dot(dqkv, r.weights[...].reshape(width, 3 * HD), NT).astype(BF16)

        def narrow(g):
            at = pl.ds(pl.multiple_of(g * 16, 16), 16)
            src = jnp.concatenate([r.wide[at, h * HD : (h + 1) * HD] for h in range(heads)], axis=0)
            part = dot(to_patches, src).astype(BF16)
            for n in range(at_once):
                r.grad0[g * at_once + n] = part[n * line : (n + 1) * line]

        loop(0, n_seq // at_once, narrow)
        j.grad.start()
        j.grad.push()
        scaled = j.grad.landed().reshape(own, heads, HD) * gn[...][None]
        unit = r.unit[...].reshape(own, heads, HD)
        inv_std = r.inv[...].reshape(own, heads, HD)
        d_pooled = inv_std * (scaled - mean(scaled) - unit * mean(scaled * unit))
        r.dp_own[...] = d_pooled.astype(BF16).reshape(line, HD)
        j.d_pooled.start()
        j.d_pooled.middle()
        j.d_pooled.landed()

        for g in range(groups):
            src = r.dp_all[g * at_once : (g + 1) * at_once].reshape(tall, HD)
            r.stack[g] = dot(to_heads, src).astype(BF16)
        for h in range(heads):
            here = slice(h * 16, (h + 1) * 16)
            part = jnp.concatenate([r.stack[g, here, :] for g in range(groups)], axis=0)
            part = dot(part, r.value_all[h], NT).astype(BF16)
            for g in range(groups):
                r.d_summary[g, here, :] = part[g * 16 : (g + 1) * 16]
        for g in range(groups):
            cross = dot(r.d_summary[g], t_group(g), NT).reshape(heads, 16, lanes)
            dmix = jnp.sum(jnp.where(wide_mask[None], cross, 0.0), axis=1)
            for o in range(octets):
                r.dmix0[g * octets + o] = dmix[o * 8 : (o + 1) * 8]
        j.dmix.start()
        for g in range(groups):
            part = dot(r.mix_tall[g], r.d_summary[g]).astype(BF16)
            r.back_b[:, :, g * 16 : (g + 1) * 16, :] = part.reshape(n_var, per, 16, cut)
        j.dmix.push()
        j.back.far(4)
        dmix = j.dmix.landed()
        mixw = r.mix[i]
        dscore = mixw * (dmix - over_vars(jnp.add, mixw * dmix)) * factor
        r.dscore_own[...] = dscore.astype(BF16).astype(F32)
        j.dscore.start()
        j.back.near(4)
        j.dscore.middle()
        j.dscore.landed()

        query_part = jnp.zeros((heads, cut), F32)
        mine = jnp.zeros((heads, per * rows), F32)
        lane, column = iota((lanes, per * rows), 0) - i * chunk, iota((lanes, per * rows), 1)
        for g in range(groups):
            dscore = r.dscore_all[g * octets : (g + 1) * octets].reshape(heads, lanes).astype(BF16)
            query_part = query_part + dot(dscore, t_group(g))
            at_lane = column // rows * 16 + lax.rem(column, 16)
            here = (lane == at_lane) & (lax.rem(column, rows) // 16 == g)
            mine = mine + dot(dscore, ones(here))
        r.query_part[...] = query_part
        j.query_z.start()
        r.dscore[...] = mine.astype(BF16)
        r.query_line[...] = j.query_z.landed()
        j.query_x.start()
        r.query_done[...] = j.query_x.landed()
        j.query.start()
        j.query.middle()
        for job in (j.tokens, j.pooled, j.normed, *ring, j.kv, j.dkv, j.grad, j.d_pooled, j.dmix, j.dscore):
            job.sent()
        j.query_z.sent()
        j.query_x.sent()
        j.query.landed()
        j.query.sent()
        j.back.landed()
        j.back.sent()

    in_vmem = pl.BlockSpec(memory_space=pltpu.VMEM)
    return pl.pallas_call(
        kernel,
        name="encoder",
        out_shape=[jax.ShapeDtypeStruct(*results[name]) for name in results],
        in_specs=[in_vmem] * 8,
        out_specs=[in_vmem] * len(results),
        scratch_shapes=[pltpu.VMEM(*buffers[name]) for name in buffers]
        + [sem for wanted in job_sems for sem in wanted],
        compiler_params=pltpu.CompilerParams(
            collective_id=0, has_side_effects=True, vmem_limit_bytes=60 * 1024 * 1024
        ),
    )(tokens, agg_query, agg_value, w_query, w_key, w_value, gain, grad_out)


def per_device(n_var, n_seq, tokens, agg_query, agg_value, w_query, w_key, w_value, gain, d_out):
    heads = agg_query.shape[0]
    attended, mixed, dscore, d_query = program(
        n_var, n_seq, tokens, agg_query, agg_value, w_query, w_key, w_value,
        gain.reshape(heads, HD), d_out.reshape(-1, HD),
    )
    through_scores = dot(dscore, agg_query, TN).reshape(tokens.shape)
    d_tokens = (mixed.astype(F32) + through_scores).astype(BF16)
    return (attended.reshape(d_out.shape), d_tokens, d_query)


def solution(mesh):
    return jax.shard_map(
        functools.partial(per_device, mesh.shape[VAR], mesh.shape[SEQ]),
        mesh=mesh,
        in_specs=(
            P(VAR, SEQ, None),
            P(),
            P(VAR, SEQ),
            P(VAR, SEQ),
            P(VAR, SEQ),
            P(VAR, SEQ),
            P(),
            P(None, VAR, SEQ),
        ),
        out_specs=(P(None, VAR, SEQ), P(VAR, SEQ, None), P()),
        check_vma=False,
    )
```

```python
import functools
from types import SimpleNamespace

import jax
import jax.numpy as jnp
from jax import lax
from jax.experimental import pallas as pl
from jax.experimental.pallas import tpu as pltpu
from jax.sharding import PartitionSpec as P

HD = 128
EPS = 1e-05
NZ = 8
MESH = pl.DeviceIdType.MESH
F32 = jnp.float32
BF16 = jnp.bfloat16
VAR, SEQ = "var", "seq"
NT = ((1,), (1,))
TN = ((0,), (0,))


def remote(src, dst, send, recv, device):
    return pltpu.make_async_remote_copy(
        src_ref=src, dst_ref=dst, send_sem=send, recv_sem=recv, device_id=device, device_id_type=MESH
    )


def loop(first, last, body):
    def step(k, carry):
        body(k)
        return carry

    lax.fori_loop(first, last, step, 0)


def slot(ref, j):
    return ref.at[j]


def dma(*shape):
    return pltpu.SemaphoreType.DMA(shape)


def first_blocks(ref, n):
    return ref.at[pl.ds(0, n)]


def arrived(ref, sem):
    remote(ref, ref, sem, sem, {}).wait_recv()


def left(ref, sem):
    remote(ref, ref, sem, sem, {}).wait_send()


class Direct:
    def __init__(self, axis, n, src=slot, dst=slot, blocks=first_blocks):
        self.axis, self.n, self.src, self.dst, self.blocks = axis, n, src, dst, blocks

    def sems(self):
        return [dma(), dma(), dma()]

    def peers(self):
        me = lax.axis_index(self.axis)
        return [(self.n - 1, lambda k: {self.axis: lax.rem(me + k + 1, self.n)})]

    def send(self, x, o, sems, k):
        me = lax.axis_index(self.axis)
        to = lax.rem(me + k, self.n)
        remote(self.src(x, to), self.dst(o, me), sems[0], sems[1], {self.axis: to}).start()

    def own(self, x, o, sems):
        me = lax.axis_index(self.axis)
        return pltpu.make_async_copy(self.src(x, me), self.dst(o, me), sems[2])

    def start(self, x, o, sems):
        loop(1, self.n, lambda k: self.send(x, o, sems, k))
        self.own(x, o, sems).start()

    def some(self, x, o, sems, *offsets):
        for k in offsets:
            if k == 0:
                self.own(x, o, sems).start()
            else:
                self.send(x, o, sems, k)
                if 2 * k != self.n:
                    self.send(x, o, sems, self.n - k)

    def landed(self, x, o, sems):
        self.own(x, o, sems).wait()
        arrived(self.blocks(o, self.n - 1), sems[1])

    def sent(self, x, o, sems):
        left(self.blocks(o, self.n - 1), sems[0])


class GatherSeq:
    def __init__(self, n):
        self.nz = NZ
        self.nx = n // NZ

    def sems(self):
        return [dma(), dma(self.nz), dma(), dma(self.nx), dma()]

    def place(self):
        me = lax.axis_index(SEQ)
        return me, me // self.nz, lax.rem(me, self.nz)

    def peers(self):
        me, x, z = self.place()
        return [
            (self.nz - 1, lambda k: {SEQ: x * self.nz + lax.rem(z + k + 1, self.nz)}),
            (self.nx - 1, lambda k: {SEQ: lax.rem(x + k + 1, self.nx) * self.nz + z}),
        ]

    def along_z(self, a, o, sems, k, received):
        me, x, z = self.place()
        at = lax.rem(z + self.nz - k, self.nz) if received else z
        return remote(
            a, o.at[x * self.nz + at], sems[0], sems[1].at[k],
            {SEQ: x * self.nz + lax.rem(z + k, self.nz)},
        )

    def along_x(self, a, o, sems, k, m):
        me, x, z = self.place()
        at = x * self.nz + lax.rem(z + self.nz - k, self.nz)
        src = a if isinstance(k, int) and k == 0 else o.at[at]
        to = lax.rem(x + m, self.nx) * self.nz + z
        remote(src, o.at[at], sems[2], sems[3].at[m], {SEQ: to}).start()

    def own(self, a, o, sems):
        return pltpu.make_async_copy(a, o.at[lax.axis_index(SEQ)], sems[4])

    def start(self, a, o, sems):
        loop(1, self.nz, lambda k: self.along_z(a, o, sems, k, False).start())
        loop(1, self.nx, lambda m: self.along_x(a, o, sems, 0, m))
        self.own(a, o, sems).start()

    def middle(self, a, o, sems):
        def forward(k):
            self.along_z(a, o, sems, k, True).wait_recv()
            loop(1, self.nx, lambda m: self.along_x(a, o, sems, k, m))

        loop(1, self.nz, forward)

    def landed(self, a, o, sems):
        self.own(a, o, sems).wait()
        loop(1, self.nx, lambda m: arrived(first_blocks(o, self.nz), sems[3].at[m]))

    def sent(self, a, o, sems):
        left(first_blocks(o, self.nz - 1), sems[0])
        left(first_blocks(o, self.nz * (self.nx - 1)), sems[2])


class GatherVar:
    def __init__(self, n, dst=slot, blocks=first_blocks):
        self.n, self.ny, self.dst, self.blocks = n, n // 2, dst, blocks

    def sems(self):
        return [dma(), dma(self.ny), dma(), dma(), dma()]

    def place(self):
        me = lax.axis_index(VAR)
        return me, me // 2, lax.rem(me, 2)

    def far(self, src, o, sems, block, way, k):
        me, y, c = self.place()
        at = 2 * lax.rem(y + self.ny - block, self.ny) + c
        src = self.dst(o, at) if src is None else src
        return remote(
            src, self.dst(o, at), sems[0], sems[1].at[k], {VAR: 2 * lax.rem(y + way, self.ny) + c}
        )

    def arrived(self, a, o, sems, k):
        me, y, c = self.place()
        arrived(self.dst(o, 2 * lax.rem(y + self.ny - k, self.ny) + c), sems[1].at[k])

    def across(self, o, sems, k, first=None):
        me, y, c = self.place()
        at = self.dst(o, 2 * lax.rem(y + self.ny - k, self.ny) + c)
        remote(at if first is None else first, at, sems[2], sems[3], {VAR: 2 * y + 1 - c}).start()

    def own(self, a, o, sems):
        return pltpu.make_async_copy(a, self.dst(o, lax.axis_index(VAR)), sems[4])

    def begin(self, a, o, sems):
        loop(1, self.ny, lambda k: self.far(a, o, sems, 0, k, k).start())

    def start(self, a, o, sems):
        self.begin(a, o, sems)
        self.across(o, sems, 0, a)
        self.own(a, o, sems).start()

    def middle(self, a, o, sems):
        def forward(k):
            self.arrived(a, o, sems, k)
            self.across(o, sems, k)

        loop(1, self.ny, forward)

    def landed(self, a, o, sems):
        self.own(a, o, sems).wait()
        arrived(self.blocks(o, self.ny), sems[3])

    def sent(self, a, o, sems):
        left(self.blocks(o, self.ny - 1), sems[0])
        left(self.blocks(o, self.ny), sems[2])


class RingVar(GatherVar):
    def begin(self, a, o, sems):
        self.far(a, o, sems, 0, 1, 1).start()
        self.far(a, o, sems, 0, self.ny - 1, self.ny - 1).start()

    def step(self, a, o, sems, t):
        half = self.ny // 2
        self.arrived(a, o, sems, t)
        if t < half:
            self.far(None, o, sems, t, 1, t + 1).start()
        self.across(o, sems, t)
        if t < half:
            self.arrived(a, o, sems, self.ny - t)
            if t < half - 1:
                self.far(None, o, sems, self.ny - t, self.ny - 1, self.ny - t - 1).start()
            self.across(o, sems, self.ny - t)


class TwoStepVar(GatherVar):
    def begin(self, a, o, sems):
        for k in (2, 6, 1, 7):
            self.far(a, o, sems, 0, k, k).start()

    def opposite(self, o, sems):
        me, y, c = self.place()
        return self.far(None, o, sems, 2 + 4 * c, 2 + 4 * c, 4)

    def middle(self, a, o, sems):
        me, y, c = self.place()
        self.arrived(a, o, sems, 2)
        self.arrived(a, o, sems, 6)
        self.opposite(o, sems).start()
        self.far(None, o, sems, 2, 1, 3).start()
        self.far(None, o, sems, 6, 7, 5).start()
        for k in (2, 6):
            self.across(o, sems, k)
        for k in (1, 7, 3, 5, 4):
            self.arrived(a, o, sems, k)
            self.across(o, sems, k)


class ReduceVar:
    def __init__(self, n):
        self.n, self.ny = n, n // 2

    def sems(self):
        return [dma(), dma(self.ny), dma(), dma()]

    def place(self):
        me = lax.axis_index(VAR)
        return me // 2, lax.rem(me, 2)

    def across(self, b, held, sems, k):
        y, c = self.place()
        yy = lax.rem(y + k + 1, self.ny)
        return remote(b.at[2 * yy + 1 - c], held.at[yy], sems[0], sems[1].at[k], {VAR: 2 * y + 1 - c})

    def along_y(self, summed, landed, sems, k):
        y, c = self.place()
        yy = lax.rem(y + k + 1, self.ny)
        remote(summed.at[yy], landed.at[y], sems[2], sems[3], {VAR: 2 * yy + c}).start()

    def start(self, b, held, summed, landed, sems):
        loop(0, self.ny, lambda k: self.across(b, held, sems, k).start())

    def push(self, b, held, summed, landed, sems):
        y, c = self.place()

        def add(k):
            yy = lax.rem(y + k + 1, self.ny)
            self.across(b, held, sems, k).wait_recv()
            total = b[2 * yy + c].astype(F32) + held[yy].astype(F32)
            summed[yy] = total.astype(summed.dtype)

        def step(k):
            add(k)
            self.along_y(summed, landed, sems, k)

        loop(0, self.ny - 1, step)
        add(self.ny - 1)

    def landed(self, b, held, summed, landed, sems):
        y, c = self.place()
        total = summed[y].astype(F32)
        arrived(first_blocks(landed, self.ny - 1), sems[3])
        for k in range(self.ny - 1):
            total = total + landed[lax.rem(y + self.ny - k - 1, self.ny)].astype(F32)
        return total

    def sent(self, b, held, summed, landed, sems):
        left(first_blocks(b, self.ny), sems[0])
        left(first_blocks(landed, self.ny - 1), sems[2])


class ReduceSeq:
    def __init__(self, n):
        self.nz, self.nx = NZ, n // NZ

    def sems(self):
        return [dma(), dma(self.nz), dma(), dma()]

    def place(self):
        me = lax.axis_index(SEQ)
        return me // self.nz, lax.rem(me, self.nz)

    def along_x(self, b, held, sems, k, m):
        x, z = self.place()
        zz = lax.rem(z + k + 1, self.nz)
        to = lax.rem(x + m, self.nx)
        remote(
            b.at[to * self.nz + zz], held.at[x * self.nz + zz], sems[0], sems[1].at[k], {SEQ: to * self.nz + z}
        ).start()

    def along_z(self, summed, landed, sems, k):
        x, z = self.place()
        zz = lax.rem(z + k + 1, self.nz)
        remote(summed.at[zz], landed.at[z], sems[2], sems[3], {SEQ: x * self.nz + zz}).start()

    def start(self, b, held, summed, landed, sems):
        def send(k):
            loop(1, self.nx, lambda m: self.along_x(b, held, sems, k, m))

        loop(0, self.nz, send)

    def push(self, b, held, summed, landed, sems):
        x, z = self.place()

        def add(k):
            zz = lax.rem(z + k + 1, self.nz)
            total = b[x * self.nz + zz].astype(F32)
            arrived(first_blocks(held, self.nx - 1), sems[1].at[k])
            for m in range(1, self.nx):
                total = total + held[lax.rem(x + self.nx - m, self.nx) * self.nz + zz].astype(F32)
            summed[zz] = total.astype(summed.dtype)

        def step(k):
            add(k)
            self.along_z(summed, landed, sems, k)

        loop(0, self.nz - 1, step)
        add(self.nz - 1)

    def landed(self, b, held, summed, landed, sems):
        x, z = self.place()
        total = summed[z].astype(F32)
        arrived(first_blocks(landed, self.nz - 1), sems[3])
        for k in range(self.nz - 1):
            total = total + landed[lax.rem(z + self.nz - k - 1, self.nz)].astype(F32)
        return total

    def sent(self, b, held, summed, landed, sems):
        left(first_blocks(b, self.nz * (self.nx - 1)), sems[0])
        left(first_blocks(landed, self.nz - 1), sems[2])


class SumAlong:
    def __init__(self, n, along_z):
        self.n, self.along_z = (NZ if along_z else n // NZ), along_z

    def sems(self):
        return [dma(), dma()]

    def place(self):
        me = lax.axis_index(SEQ)
        return lax.rem(me, NZ) if self.along_z else me // NZ

    def send(self, src, held, sems, k):
        me = lax.axis_index(SEQ)
        to = lax.rem(self.place() + k, self.n)
        to = me // NZ * NZ + to if self.along_z else to * NZ + lax.rem(me, NZ)
        remote(src, held.at[self.place()], sems[0], sems[1], {SEQ: to}).start()

    def start(self, src, held, sems):
        loop(1, self.n, lambda k: self.send(src, held, sems, k))
        held[self.place()] = src[...]

    def landed(self, src, held, sems):
        arrived(first_blocks(held, self.n - 1), sems[1])
        total = held[0]
        for at in range(1, self.n):
            total = total + held[at]
        return total

    def sent(self, src, held, sems):
        left(first_blocks(held, self.n - 1), sems[0])


def bound(job, sems, refs):
    def fill(phase):
        return lambda *more: phase(*refs, sems, *more)

    return SimpleNamespace(
        **{name: fill(getattr(job, name)) for name in dir(job) if not name.startswith("_") and name != "n"
           and callable(getattr(job, name))}
    )


def barrier(groups):
    sem = pltpu.get_barrier_semaphore()
    for count, to in groups:
        loop(0, count, lambda k: pl.semaphore_signal(sem, inc=1, device_id=to(k), device_id_type=MESH))
    return lambda: pl.semaphore_wait(sem, sum(count for count, _ in groups))


def dot(a, b, dims=((1,), (0,))):
    return lax.dot_general(a, b, (dims, ((), ())), preferred_element_type=F32)


def over_vars(fold, z):
    out = z[:, :128]
    for at in range(128, z.shape[1], 128):
        out = fold(out, z[:, at : at + 128])
    for shift in (64, 32, 16):
        out = fold(out, pltpu.roll(out, shift, 1))
    return jnp.concatenate([out] * (z.shape[1] // 128), axis=1)


def program(n_var, n_seq, tokens, agg_query, agg_value, w_query, w_key, w_value, gain, grad_out):
    factor = HD ** (-0.5)
    per, rows, width = tokens.shape
    heads = agg_query.shape[0]
    octets = heads // 8
    cut = width // n_var
    own = rows // n_var
    line = own * heads
    groups = rows // 16
    chunk = per * 16
    lanes = n_var * chunk
    tall = 16 * heads
    row_count = n_seq * own
    at_once = 16 // own
    ny, nz, nx = n_var // 2, NZ, n_seq // NZ

    at_cut = lambda j: pl.ds(pl.multiple_of(j * cut, cut), cut)
    weight = lambda w: RingVar(
        n_var, lambda o, j: o.at[j, :, pl.ds(w * HD, HD)], lambda o, n: o.at[pl.ds(0, n), :, pl.ds(w * HD, HD)]
    )
    jobs = dict(
        tokens=Direct(VAR, n_var, lambda x, j: x.at[:, :, at_cut(j)], slot),
        scores=GatherVar(n_var),
        value=GatherSeq(n_seq),
        pooled=ReduceVar(n_var),
        normed=GatherSeq(n_seq),
        w_query=weight(0),
        w_key=weight(1),
        w_value=weight(2),
        kv=TwoStepVar(n_var),
        dkv=ReduceVar(n_var),
        grad=ReduceSeq(n_seq),
        d_pooled=GatherVar(n_var),
        dmix=ReduceVar(n_var),
        dscore=GatherVar(n_var),
        back=Direct(VAR, n_var, slot, lambda o, j: o.at[:, :, at_cut(j)], lambda o, n: o.at[:, :, pl.ds(0, n * cut)]),
        query_z=SumAlong(n_seq, True),
        query_x=SumAlong(n_seq, False),
        query=GatherVar(n_var, lambda o, j: o.at[:, at_cut(j)], lambda o, n: o.at[:, pl.ds(0, n * cut)]),
    )

    block = lambda n, r=line, c=HD, t=BF16: ((n, r, c), t)

    def through(blocks, *rest):
        return block(blocks, *rest), block(ny, *rest), block(ny, *rest), block(ny, *rest)

    pooled, dkv = through(n_var), through(n_var, row_count, 2 * HD)
    dmix = through(n_var, 8, lanes, F32)
    buffers = dict(
        grouped=((n_var, per, rows, cut), BF16),
        s_own=((heads, 256), F32),
        s_all=block(n_var, heads, 256, F32),
        value_all=block(n_seq, cut, HD),
        mix=block(n_var, 8, lanes, F32),
        mix_wide=block(groups, tall, lanes),
        mix_tall=block(groups, lanes, tall),
        summary=block(groups, tall, cut),
        stack=block(groups, tall, HD),
        pooled0=pooled[0], pooled1=pooled[1], pooled2=pooled[2], pooled3=pooled[3],
        unit=((line, HD), F32),
        inv=((line, HD), F32),
        normed_own=((line, HD), BF16),
        normed_all=block(n_seq),
        weights=block(n_var, cut, 3 * HD),
        wide=((row_count, width), BF16),
        kv_own=((row_count, 2 * HD), BF16),
        kv_all=block(n_var, row_count, 2 * HD),
        dkv0=dkv[0], dkv1=dkv[1], dkv2=dkv[2], dkv3=dkv[3],
        grad0=block(n_seq), grad1=block(n_seq), grad2=block(nz), grad3=block(nz),
        dp_own=((line, HD), BF16),
        dp_all=block(n_var),
        d_summary=block(groups, tall, cut),
        dmix0=dmix[0], dmix1=dmix[1], dmix2=dmix[2], dmix3=dmix[3],
        dscore_own=((16, lanes // 2), BF16),
        dscore_all=block(n_var, 16, lanes // 2),
        back_b=((n_var, per, rows, cut), BF16),
        query_part=((heads, cut), F32),
        query_line=((heads, cut), F32),
        query_done=((heads, cut), F32),
        query_z=block(nz, heads, cut, F32),
        query_x=block(nx, heads, cut, F32),
    )
    results = dict(
        attended=((row_count, HD), BF16),
        mixed=(tokens.shape, BF16),
        dscore=((heads, per * rows), BF16),
        d_query=((heads, width), F32),
    )
    names = [*results, *buffers]
    job_sems = [job.sems() for job in jobs.values()]

    def kernel(tok, aq, av, wq, wk, wv, gn, go, *rest):
        r = SimpleNamespace(**dict(zip(names, rest)))
        refs = dict(
            tokens=(tok, r.grouped),
            scores=(r.s_own, r.s_all),
            value=(av, r.value_all),
            pooled=(r.pooled0, r.pooled1, r.pooled2, r.pooled3),
            normed=(r.normed_own, r.normed_all),
            w_query=(wq, r.weights),
            w_key=(wk, r.weights),
            w_value=(wv, r.weights),
            kv=(r.kv_own, r.kv_all),
            dkv=(r.dkv0, r.dkv1, r.dkv2, r.dkv3),
            grad=(r.grad0, r.grad1, r.grad2, r.grad3),
            d_pooled=(r.dp_own, r.dp_all),
            dmix=(r.dmix0, r.dmix1, r.dmix2, r.dmix3),
            dscore=(r.dscore_own, r.dscore_all),
            back=(r.back_b, r.mixed),
            query_z=(r.query_part, r.query_z),
            query_x=(r.query_line, r.query_x),
            query=(r.query_done, r.d_query),
        )
        left, ready_jobs = list(rest[len(names) :]), {}
        for (name, job), wanted in zip(jobs.items(), job_sems):
            ready_jobs[name] = bound(job, left[: len(wanted)], refs[name])
            left = left[len(wanted) :]
        j = SimpleNamespace(**ready_jobs)
        ring = (j.w_key, j.w_value, j.w_query)

        def t_group(g):
            return r.grouped[:, :, g * 16 : (g + 1) * 16, :].reshape(lanes, cut)

        i = lax.axis_index(VAR)
        greeted = barrier(jobs["tokens"].peers() + jobs["value"].peers())

        rows_here = [tok[v, g * 16 : (g + 1) * 16, :] for g in range(groups) for v in range(per)]
        local = dot(aq[...], jnp.concatenate(rows_here, axis=0), NT) * factor
        r.s_own[...] = jnp.concatenate([local, jnp.zeros((heads, 256 - per * rows), F32)], axis=1)
        greeted()
        j.scores.start()
        j.value.start()
        j.tokens.start()
        j.scores.middle()
        j.value.middle()

        iota = lambda shape, dim: lax.broadcasted_iota(jnp.int32, shape, dim)
        ones = lambda where: where.astype(F32).astype(BF16)
        wide_mask = lax.rem(iota((16, lanes), 1), 16) == iota((16, lanes), 0)
        tall_mask = lax.rem(iota((lanes, tall), 0), 16) == lax.rem(iota((lanes, tall), 1), 16)
        spread_heads = ones(iota((heads, tall), 1) // 16 == iota((heads, tall), 0))
        at, to = iota((tall, tall), 0), iota((tall, tall), 1)
        to_patches = ones(to == lax.rem(at, heads) * 16 + at // heads)
        to_heads = ones(to == lax.rem(at, 16) * heads + at // 16)

        j.scores.landed()
        for g in range(groups):
            z = jnp.concatenate([r.s_all[n, :, g * chunk : (g + 1) * chunk] for n in range(n_var)], axis=1)
            e = jnp.exp(z - over_vars(jnp.maximum, z))
            mixw = e / over_vars(jnp.add, e)
            for o in range(octets):
                r.mix[g * octets + o] = mixw[o * 8 : (o + 1) * 8]
            mix_b = mixw.astype(BF16)
            full = jnp.broadcast_to(mix_b.astype(F32)[:, None, :], (heads, 16, lanes))
            full = jnp.where(wide_mask[None], full, 0.0)
            r.mix_wide[g] = full.astype(BF16).reshape(tall, lanes)
            r.mix_tall[g] = jnp.where(tall_mask, dot(mix_b, spread_heads, TN), 0.0).astype(BF16)
        j.value.landed()
        j.scores.sent()
        j.value.sent()
        j.tokens.landed()
        for w in ring:
            w.start()

        for g in range(groups):
            r.summary[g] = dot(r.mix_wide[g], t_group(g)).astype(BF16)
        for h in range(heads):
            here = slice(h * 16, (h + 1) * 16)
            part = jnp.concatenate([r.summary[g, here, :] for g in range(groups)], axis=0)
            part = dot(part, r.value_all[h]).astype(BF16)
            for g in range(groups):
                r.stack[g, here, :] = part[g * 16 : (g + 1) * 16]
        for g in range(groups):
            part = dot(to_patches, r.stack[g]).astype(BF16)
            for n in range(at_once):
                r.pooled0[g * at_once + n] = part[n * line : (n + 1) * line]
        j.pooled.start()
        j.pooled.push()
        for w in ring:
            w.step(1)
        pooled = j.pooled.landed().astype(BF16).astype(F32).reshape(own, heads, HD)
        mean = lambda a: jnp.sum(jnp.sum(a, axis=1, keepdims=True), axis=2, keepdims=True) / width
        center = mean(pooled)
        inv_std = lax.rsqrt(mean((pooled - center) ** 2) + EPS)
        unit = (pooled - center) * inv_std
        r.normed_own[...] = (unit * gn[...][None]).astype(BF16).reshape(line, HD)
        j.normed.start()
        r.unit[...] = unit.reshape(line, HD)
        r.inv[...] = jnp.broadcast_to(inv_std, (own, heads, HD)).reshape(line, HD)
        for w in ring:
            w.step(2)
        j.normed.middle()
        for t in range(3, ny // 2 + 1):
            for w in ring:
                w.step(t)
        j.normed.landed()

        def widen(g):
            src = r.normed_all[pl.ds(g * at_once, at_once)].reshape(tall, HD)
            part = dot(to_heads, src).astype(BF16)
            for h in range(heads):
                r.wide[pl.ds(pl.multiple_of(g * 16, 16), 16), h * HD : (h + 1) * HD] = part[h * 16 : (h + 1) * 16]

        loop(0, n_seq // at_once, widen)
        j.w_key.landed()
        j.w_value.landed()
        kv_weights = r.weights[:, :, HD:].reshape(width, 2 * HD)
        r.kv_own[...] = dot(r.wide[...], kv_weights).astype(BF16)
        j.kv.start()
        j.w_query.landed()
        queries = dot(r.wide[...], r.weights[:, :, :HD].reshape(width, HD)).astype(BF16)
        j.kv.middle()
        j.kv.landed()

        keys = r.kv_all[:, :, :HD].reshape(n_var * row_count, HD)
        values = r.kv_all[:, :, HD:].reshape(n_var * row_count, HD)
        grad = go[...]
        logits = dot(queries, keys, NT) * factor
        expo = jnp.exp(logits - jnp.max(logits, axis=1, keepdims=True))
        probs = expo / jnp.sum(expo, axis=1, keepdims=True)
        probs_b = probs.astype(BF16)
        dprob = dot(grad, values, NT)
        dlogit = (probs * (dprob - jnp.sum(probs * dprob, axis=1, keepdims=True)) * factor).astype(BF16)
        r.dkv0[:, :, :HD] = dot(dlogit, queries, TN).astype(BF16).reshape(n_var, row_count, HD)
        r.dkv0[:, :, HD:] = dot(probs_b, grad, TN).astype(BF16).reshape(n_var, row_count, HD)
        j.dkv.start()
        r.attended[...] = dot(probs_b, values).astype(BF16)
        dquery = dot(dlogit, keys).astype(BF16)
        j.dkv.push()
        dkv = j.dkv.landed().astype(BF16)

        dqkv = jnp.concatenate([dquery, dkv], axis=1)
        r.wide[...] = dot(dqkv, r.weights[...].reshape(width, 3 * HD), NT).astype(BF16)

        def narrow(g):
            at = pl.ds(pl.multiple_of(g * 16, 16), 16)
            src = jnp.concatenate([r.wide[at, h * HD : (h + 1) * HD] for h in range(heads)], axis=0)
            part = dot(to_patches, src).astype(BF16)
            for n in range(at_once):
                r.grad0[g * at_once + n] = part[n * line : (n + 1) * line]

        loop(0, n_seq // at_once, narrow)
        j.grad.start()
        j.grad.push()
        scaled = j.grad.landed().reshape(own, heads, HD) * gn[...][None]
        unit = r.unit[...].reshape(own, heads, HD)
        inv_std = r.inv[...].reshape(own, heads, HD)
        d_pooled = inv_std * (scaled - mean(scaled) - unit * mean(scaled * unit))
        r.dp_own[...] = d_pooled.astype(BF16).reshape(line, HD)
        j.d_pooled.start()
        j.d_pooled.middle()
        j.d_pooled.landed()

        for g in range(groups):
            src = r.dp_all[g * at_once : (g + 1) * at_once].reshape(tall, HD)
            r.stack[g] = dot(to_heads, src).astype(BF16)
        for h in range(heads):
            here = slice(h * 16, (h + 1) * 16)
            part = jnp.concatenate([r.stack[g, here, :] for g in range(groups)], axis=0)
            part = dot(part, r.value_all[h], NT).astype(BF16)
            for g in range(groups):
                r.d_summary[g, here, :] = part[g * 16 : (g + 1) * 16]
        for g in range(groups):
            cross = dot(r.d_summary[g], t_group(g), NT).reshape(heads, 16, lanes)
            dmix = jnp.sum(jnp.where(wide_mask[None], cross, 0.0), axis=1)
            for o in range(octets):
                r.dmix0[g * octets + o] = dmix[o * 8 : (o + 1) * 8]
        j.dmix.start()
        for g in range(groups):
            part = dot(r.mix_tall[g], r.d_summary[g]).astype(BF16)
            r.back_b[:, :, g * 16 : (g + 1) * 16, :] = part.reshape(n_var, per, 16, cut)
        j.dmix.push()
        j.back.some(0, 1, 2)
        dmix = j.dmix.landed()
        mixw = r.mix[i]
        dscore = mixw * (dmix - over_vars(jnp.add, mixw * dmix)) * factor
        r.dscore_own[...] = jnp.concatenate([dscore[:, : lanes // 2], dscore[:, lanes // 2 :]], axis=0).astype(BF16)
        j.dscore.start()
        j.back.some(3)
        j.dscore.middle()
        j.dscore.landed()
        j.back.some(7, 6)

        query_part = jnp.zeros((heads, cut), F32)
        mine = jnp.zeros((heads, per * rows), F32)
        lane, column = iota((lanes, per * rows), 0) - i * chunk, iota((lanes, per * rows), 1)
        for g in range(groups):
            halves = r.dscore_all[g * octets : (g + 1) * octets].astype(F32)
            dscore = jnp.concatenate([halves[:, :8], halves[:, 8:]], axis=2).reshape(heads, lanes).astype(BF16)
            query_part = query_part + dot(dscore, t_group(g))
            at_lane = column // rows * 16 + lax.rem(column, 16)
            here = (lane == at_lane) & (lax.rem(column, rows) // 16 == g)
            mine = mine + dot(dscore, ones(here))
        r.query_part[...] = query_part
        j.query_z.start()
        r.dscore[...] = mine.astype(BF16)
        r.query_line[...] = j.query_z.landed()
        j.query_x.start()
        r.query_done[...] = j.query_x.landed()
        j.query.start()
        j.back.some(8, 5, 4)
        j.query.middle()
        for job in (j.tokens, j.pooled, j.normed, *ring, j.kv, j.dkv, j.grad, j.d_pooled, j.dmix, j.dscore):
            job.sent()
        j.query_z.sent()
        j.query_x.sent()
        j.query.landed()
        j.query.sent()
        j.back.landed()
        j.back.sent()

    in_vmem = pl.BlockSpec(memory_space=pltpu.VMEM)
    return pl.pallas_call(
        kernel,
        name="encoder",
        out_shape=[jax.ShapeDtypeStruct(*results[name]) for name in results],
        in_specs=[in_vmem] * 8,
        out_specs=[in_vmem] * len(results),
        scratch_shapes=[pltpu.VMEM(*buffers[name]) for name in buffers]
        + [sem for wanted in job_sems for sem in wanted],
        compiler_params=pltpu.CompilerParams(
            collective_id=0, has_side_effects=True, vmem_limit_bytes=60 * 1024 * 1024
        ),
    )(tokens, agg_query, agg_value, w_query, w_key, w_value, gain, grad_out)


def per_device(n_var, n_seq, tokens, agg_query, agg_value, w_query, w_key, w_value, gain, d_out):
    heads = agg_query.shape[0]
    attended, mixed, dscore, d_query = program(
        n_var, n_seq, tokens, agg_query, agg_value, w_query, w_key, w_value,
        gain.reshape(heads, HD), d_out.reshape(-1, HD),
    )
    through_scores = dot(dscore, agg_query, TN).reshape(tokens.shape)
    d_tokens = (mixed.astype(F32) + through_scores).astype(BF16)
    return (attended.reshape(d_out.shape), d_tokens, d_query)


def solution(mesh):
    return jax.shard_map(
        functools.partial(per_device, mesh.shape[VAR], mesh.shape[SEQ]),
        mesh=mesh,
        in_specs=(
            P(VAR, SEQ, None),
            P(),
            P(VAR, SEQ),
            P(VAR, SEQ),
            P(VAR, SEQ),
            P(VAR, SEQ),
            P(),
            P(None, VAR, SEQ),
        ),
        out_specs=(P(None, VAR, SEQ), P(VAR, SEQ, None), P()),
        check_vma=False,
    )
```

```python
import functools
from types import SimpleNamespace

import jax
import jax.numpy as jnp
from jax import lax
from jax.experimental import pallas as pl
from jax.experimental.pallas import tpu as pltpu
from jax.sharding import PartitionSpec as P

HD = 128
EPS = 1e-05
NZ = 8
MESH = pl.DeviceIdType.MESH
F32 = jnp.float32
BF16 = jnp.bfloat16
VAR, SEQ = "var", "seq"
X, Z = "x", "z"
NT = ((1,), (1,))
TN = ((0,), (0,))


def remote(src, dst, send, recv, device):
    return pltpu.make_async_remote_copy(
        src_ref=src, dst_ref=dst, send_sem=send, recv_sem=recv, device_id=device, device_id_type=MESH
    )


def loop(first, last, body):
    def step(k, carry):
        body(k)
        return carry

    lax.fori_loop(first, last, step, 0)


def slot(ref, j):
    return ref.at[j]


def whole(ref, j):
    return ref


def dma(*shape):
    return pltpu.SemaphoreType.DMA(shape)


def first_blocks(ref, n):
    return ref.at[pl.ds(0, n)]


def arrived(ref, sem):
    remote(ref, ref, sem, sem, {}).wait_recv()


def left(ref, sem):
    remote(ref, ref, sem, sem, {}).wait_send()


class Direct:
    def __init__(self, axis, n, src=slot, dst=slot, blocks=first_blocks):
        self.axis, self.n, self.src, self.dst, self.blocks = axis, n, src, dst, blocks

    def sems(self):
        return [dma(), dma(), dma()]

    def here(self):
        if self.axis == VAR:
            return lax.axis_index(VAR)
        return lax.axis_index(SEQ) // NZ if self.axis == X else lax.rem(lax.axis_index(SEQ), NZ)

    def device(self, to):
        if self.axis == VAR:
            return {VAR: to}
        me = lax.axis_index(SEQ)
        return {SEQ: to * NZ + lax.rem(me, NZ) if self.axis == X else me // NZ * NZ + to}

    def peers(self):
        return [(self.n - 1, lambda k: self.device(lax.rem(self.here() + k + 1, self.n)))]

    def send(self, x, o, sems, k):
        me = self.here()
        to = lax.rem(me + k, self.n)
        remote(self.src(x, to), self.dst(o, me), sems[0], sems[1], self.device(to)).start()

    def own(self, x, o, sems):
        me = self.here()
        return pltpu.make_async_copy(self.src(x, me), self.dst(o, me), sems[2])

    def start(self, x, o, sems):
        loop(1, self.n, lambda k: self.send(x, o, sems, k))
        self.own(x, o, sems).start()

    def some(self, x, o, sems, *offsets):
        for k in offsets:
            if k == 0:
                self.own(x, o, sems).start()
            else:
                self.send(x, o, sems, k)
                if 2 * k != self.n:
                    self.send(x, o, sems, self.n - k)

    def landed(self, x, o, sems):
        self.own(x, o, sems).wait()
        arrived(self.blocks(o, self.n - 1), sems[1])

    def sent(self, x, o, sems):
        left(self.blocks(o, self.n - 1), sems[0])


class GatherSeq:
    def __init__(self, n):
        self.nz = NZ
        self.nx = n // NZ

    def sems(self):
        return [dma(), dma(self.nz), dma(), dma(self.nx), dma()]

    def place(self):
        me = lax.axis_index(SEQ)
        return me, me // self.nz, lax.rem(me, self.nz)

    def peers(self):
        me, x, z = self.place()
        return [
            (self.nz - 1, lambda k: {SEQ: x * self.nz + lax.rem(z + k + 1, self.nz)}),
            (self.nx - 1, lambda k: {SEQ: lax.rem(x + k + 1, self.nx) * self.nz + z}),
        ]

    def along_z(self, a, o, sems, k, received):
        me, x, z = self.place()
        at = lax.rem(z + self.nz - k, self.nz) if received else z
        return remote(
            a, o.at[x * self.nz + at], sems[0], sems[1].at[k],
            {SEQ: x * self.nz + lax.rem(z + k, self.nz)},
        )

    def along_x(self, a, o, sems, k, m):
        me, x, z = self.place()
        at = x * self.nz + lax.rem(z + self.nz - k, self.nz)
        src = a if isinstance(k, int) and k == 0 else o.at[at]
        to = lax.rem(x + m, self.nx) * self.nz + z
        remote(src, o.at[at], sems[2], sems[3].at[m], {SEQ: to}).start()

    def own(self, a, o, sems):
        return pltpu.make_async_copy(a, o.at[lax.axis_index(SEQ)], sems[4])

    def start(self, a, o, sems):
        loop(1, self.nz, lambda k: self.along_z(a, o, sems, k, False).start())
        loop(1, self.nx, lambda m: self.along_x(a, o, sems, 0, m))
        self.own(a, o, sems).start()

    def middle(self, a, o, sems):
        def forward(k):
            self.along_z(a, o, sems, k, True).wait_recv()
            loop(1, self.nx, lambda m: self.along_x(a, o, sems, k, m))

        loop(1, self.nz, forward)

    def landed(self, a, o, sems):
        self.own(a, o, sems).wait()
        loop(1, self.nx, lambda m: arrived(first_blocks(o, self.nz), sems[3].at[m]))

    def sent(self, a, o, sems):
        left(first_blocks(o, self.nz - 1), sems[0])
        left(first_blocks(o, self.nz * (self.nx - 1)), sems[2])


class GatherVar:
    def __init__(self, n, dst=slot, blocks=first_blocks):
        self.n, self.ny, self.dst, self.blocks = n, n // 2, dst, blocks

    def sems(self):
        return [dma(), dma(self.ny), dma(), dma(), dma()]

    def place(self):
        me = lax.axis_index(VAR)
        return me, me // 2, lax.rem(me, 2)

    def far(self, src, o, sems, block, way, k):
        me, y, c = self.place()
        at = 2 * lax.rem(y + self.ny - block, self.ny) + c
        src = self.dst(o, at) if src is None else src
        return remote(
            src, self.dst(o, at), sems[0], sems[1].at[k], {VAR: 2 * lax.rem(y + way, self.ny) + c}
        )

    def arrived(self, a, o, sems, k):
        me, y, c = self.place()
        arrived(self.dst(o, 2 * lax.rem(y + self.ny - k, self.ny) + c), sems[1].at[k])

    def across(self, o, sems, k, first=None):
        me, y, c = self.place()
        at = self.dst(o, 2 * lax.rem(y + self.ny - k, self.ny) + c)
        remote(at if first is None else first, at, sems[2], sems[3], {VAR: 2 * y + 1 - c}).start()

    def own(self, a, o, sems):
        return pltpu.make_async_copy(a, self.dst(o, lax.axis_index(VAR)), sems[4])

    def begin(self, a, o, sems):
        loop(1, self.ny, lambda k: self.far(a, o, sems, 0, k, k).start())

    def start(self, a, o, sems):
        self.begin(a, o, sems)
        self.across(o, sems, 0, a)
        self.own(a, o, sems).start()

    def middle(self, a, o, sems):
        def forward(k):
            self.arrived(a, o, sems, k)
            self.across(o, sems, k)

        loop(1, self.ny, forward)

    def landed(self, a, o, sems):
        self.own(a, o, sems).wait()
        arrived(self.blocks(o, self.ny), sems[3])

    def sent(self, a, o, sems):
        left(self.blocks(o, self.ny - 1), sems[0])
        left(self.blocks(o, self.ny), sems[2])


class RingVar(GatherVar):
    def begin(self, a, o, sems):
        self.far(a, o, sems, 0, 1, 1).start()
        self.far(a, o, sems, 0, self.ny - 1, self.ny - 1).start()

    def step(self, a, o, sems, t):
        half = self.ny // 2
        self.arrived(a, o, sems, t)
        if t < half:
            self.far(None, o, sems, t, 1, t + 1).start()
        self.across(o, sems, t)
        if t < half:
            self.arrived(a, o, sems, self.ny - t)
            if t < half - 1:
                self.far(None, o, sems, self.ny - t, self.ny - 1, self.ny - t - 1).start()
            self.across(o, sems, self.ny - t)


class TwoStepVar(GatherVar):
    def begin(self, a, o, sems):
        for k in (2, 6, 1, 7):
            self.far(a, o, sems, 0, k, k).start()

    def opposite(self, o, sems):
        me, y, c = self.place()
        return self.far(None, o, sems, 2 + 4 * c, 2 + 4 * c, 4)

    def middle(self, a, o, sems):
        me, y, c = self.place()
        self.arrived(a, o, sems, 2)
        self.arrived(a, o, sems, 6)
        self.opposite(o, sems).start()
        self.far(None, o, sems, 2, 1, 3).start()
        self.far(None, o, sems, 6, 7, 5).start()
        for k in (2, 6):
            self.across(o, sems, k)
        for k in (1, 7, 3, 5, 4):
            self.arrived(a, o, sems, k)
            self.across(o, sems, k)


class ReduceVar:
    def __init__(self, n):
        self.n, self.ny = n, n // 2

    def sems(self):
        return [dma(), dma(self.ny), dma(), dma()]

    def place(self):
        me = lax.axis_index(VAR)
        return me // 2, lax.rem(me, 2)

    def across(self, b, held, sems, k):
        y, c = self.place()
        yy = lax.rem(y + k + 1, self.ny)
        return remote(b.at[2 * yy + 1 - c], held.at[yy], sems[0], sems[1].at[k], {VAR: 2 * y + 1 - c})

    def along_y(self, summed, landed, sems, k):
        y, c = self.place()
        yy = lax.rem(y + k + 1, self.ny)
        remote(summed.at[yy], landed.at[y], sems[2], sems[3], {VAR: 2 * yy + c}).start()

    def start(self, b, held, summed, landed, sems):
        loop(0, self.ny, lambda k: self.across(b, held, sems, k).start())

    def push(self, b, held, summed, landed, sems):
        y, c = self.place()

        def add(k):
            yy = lax.rem(y + k + 1, self.ny)
            self.across(b, held, sems, k).wait_recv()
            total = b[2 * yy + c].astype(F32) + held[yy].astype(F32)
            summed[yy] = total.astype(summed.dtype)

        def step(k):
            add(k)
            self.along_y(summed, landed, sems, k)

        loop(0, self.ny - 1, step)
        add(self.ny - 1)

    def landed(self, b, held, summed, landed, sems):
        y, c = self.place()
        total = summed[y].astype(F32)
        arrived(first_blocks(landed, self.ny - 1), sems[3])
        for k in range(self.ny - 1):
            total = total + landed[lax.rem(y + self.ny - k - 1, self.ny)].astype(F32)
        return total

    def sent(self, b, held, summed, landed, sems):
        left(first_blocks(b, self.ny), sems[0])
        left(first_blocks(landed, self.ny - 1), sems[2])


class ReduceSeq:
    def __init__(self, n):
        self.nz, self.nx = NZ, n // NZ

    def sems(self):
        return [dma(), dma(self.nz), dma(), dma()]

    def place(self):
        me = lax.axis_index(SEQ)
        return me // self.nz, lax.rem(me, self.nz)

    def along_x(self, b, held, sems, k, m):
        x, z = self.place()
        zz = lax.rem(z + k + 1, self.nz)
        to = lax.rem(x + m, self.nx)
        remote(
            b.at[to * self.nz + zz], held.at[x * self.nz + zz], sems[0], sems[1].at[k], {SEQ: to * self.nz + z}
        ).start()

    def along_z(self, summed, landed, sems, k):
        x, z = self.place()
        zz = lax.rem(z + k + 1, self.nz)
        remote(summed.at[zz], landed.at[z], sems[2], sems[3], {SEQ: x * self.nz + zz}).start()

    def start(self, b, held, summed, landed, sems):
        def send(k):
            loop(1, self.nx, lambda m: self.along_x(b, held, sems, k, m))

        loop(0, self.nz, send)

    def push(self, b, held, summed, landed, sems):
        x, z = self.place()

        def add(k):
            zz = lax.rem(z + k + 1, self.nz)
            total = b[x * self.nz + zz].astype(F32)
            arrived(first_blocks(held, self.nx - 1), sems[1].at[k])
            for m in range(1, self.nx):
                total = total + held[lax.rem(x + self.nx - m, self.nx) * self.nz + zz].astype(F32)
            summed[zz] = total.astype(summed.dtype)

        def step(k):
            add(k)
            self.along_z(summed, landed, sems, k)

        loop(0, self.nz - 1, step)
        add(self.nz - 1)

    def landed(self, b, held, summed, landed, sems):
        x, z = self.place()
        total = summed[z].astype(F32)
        arrived(first_blocks(landed, self.nz - 1), sems[3])
        for k in range(self.nz - 1):
            total = total + landed[lax.rem(z + self.nz - k - 1, self.nz)].astype(F32)
        return total

    def sent(self, b, held, summed, landed, sems):
        left(first_blocks(b, self.nz * (self.nx - 1)), sems[0])
        left(first_blocks(landed, self.nz - 1), sems[2])


def bound(job, sems, refs):
    def fill(phase):
        return lambda *more: phase(*refs, sems, *more)

    return SimpleNamespace(
        **{name: fill(getattr(job, name)) for name in dir(job) if not name.startswith("_") and name != "n"
           and callable(getattr(job, name))}
    )


def barrier(groups):
    sem = pltpu.get_barrier_semaphore()
    for count, to in groups:
        loop(0, count, lambda k: pl.semaphore_signal(sem, inc=1, device_id=to(k), device_id_type=MESH))
    return lambda: pl.semaphore_wait(sem, sum(count for count, _ in groups))


def dot(a, b, dims=((1,), (0,))):
    return lax.dot_general(a, b, (dims, ((), ())), preferred_element_type=F32)


def over_vars(fold, z):
    out = z[:, :128]
    for at in range(128, z.shape[1], 128):
        out = fold(out, z[:, at : at + 128])
    for shift in (64, 32, 16):
        out = fold(out, pltpu.roll(out, shift, 1))
    return jnp.concatenate([out] * (z.shape[1] // 128), axis=1)


def program(n_var, n_seq, tokens, agg_query, agg_value, w_query, w_key, w_value, gain, grad_out):
    factor = HD ** (-0.5)
    per, rows, width = tokens.shape
    heads = agg_query.shape[0]
    octets = heads // 8
    cut = width // n_var
    own = rows // n_var
    line = own * heads
    groups = rows // 16
    chunk = per * 16
    lanes = n_var * chunk
    tall = 16 * heads
    row_count = n_seq * own
    at_once = 16 // own
    ny, nz, nx = n_var // 2, NZ, n_seq // NZ
    share = heads // nx

    at_cut = lambda j: pl.ds(pl.multiple_of(j * cut, cut), cut)
    few = lambda j: pl.ds(pl.multiple_of(j * share, share), share)
    weight = lambda w: RingVar(
        n_var, lambda o, j: o.at[j, :, pl.ds(w * HD, HD)], lambda o, n: o.at[pl.ds(0, n), :, pl.ds(w * HD, HD)]
    )
    jobs = dict(
        tokens=Direct(VAR, n_var, lambda x, j: x.at[:, :, at_cut(j)], slot),
        scores=GatherVar(n_var),
        value=GatherSeq(n_seq),
        pooled=ReduceVar(n_var),
        normed=GatherSeq(n_seq),
        w_query=weight(0),
        w_key=weight(1),
        w_value=weight(2),
        kv=TwoStepVar(n_var),
        dkv=ReduceVar(n_var),
        grad=ReduceSeq(n_seq),
        d_pooled=GatherVar(n_var),
        dmix=ReduceVar(n_var),
        dscore=GatherVar(n_var),
        back=Direct(VAR, n_var, slot, lambda o, j: o.at[:, at_cut(j)], lambda o, n: o.at[:, pl.ds(0, n * cut)]),
        query_z=Direct(Z, nz, whole),
        query_x=Direct(X, nx, lambda x, j: x.at[few(j)]),
        query=GatherVar(n_var, lambda o, j: o.at[:, at_cut(j)], lambda o, n: o.at[:, pl.ds(0, n * cut)]),
        query_all=Direct(X, nx, whole, lambda o, j: o.at[few(j)], lambda o, n: o.at[pl.ds(0, n * share)]),
    )

    block = lambda n, r=line, c=HD, t=BF16: ((n, r, c), t)

    def through(blocks, *rest):
        return block(blocks, *rest), block(ny, *rest), block(ny, *rest), block(ny, *rest)

    pooled, dkv = through(n_var), through(n_var, row_count, 2 * HD)
    dmix = through(n_var, 8, lanes, F32)
    buffers = dict(
        grouped=((n_var, per, rows, cut), BF16),
        s_own=((heads, (per + 1) * rows), BF16),
        s_all=block(n_var, heads, (per + 1) * rows),
        value_all=block(n_seq, cut, HD),
        mix=block(n_var, 8, lanes, F32),
        mix_wide=block(groups, tall, lanes),
        mix_tall=block(groups, lanes, tall),
        summary=block(groups, tall, cut),
        stack=block(groups, tall, HD),
        pooled0=pooled[0], pooled1=pooled[1], pooled2=pooled[2], pooled3=pooled[3],
        unit=((line, HD), F32),
        inv=((line, HD), F32),
        normed_own=((line, HD), BF16),
        normed_all=block(n_seq),
        weights=block(n_var, cut, 3 * HD),
        wide=((row_count, width), BF16),
        kv_own=((row_count, 2 * HD), BF16),
        kv_all=block(n_var, row_count, 2 * HD),
        dkv0=dkv[0], dkv1=dkv[1], dkv2=dkv[2], dkv3=dkv[3],
        grad0=block(n_seq), grad1=block(n_seq), grad2=block(nz), grad3=block(nz),
        dp_own=((line, HD), BF16),
        dp_all=block(n_var),
        d_summary=block(groups, tall, cut),
        dmix0=dmix[0], dmix1=dmix[1], dmix2=dmix[2], dmix3=dmix[3],
        dscore_own=((16, lanes // 2), BF16),
        dscore_all=block(n_var, 16, lanes // 2),
        back_b=block(n_var, per * rows, cut),
        query_part=((heads, cut), F32),
        query_line=((heads, cut), F32),
        query_done=((share, cut), F32),
        query_wide=((share, width), F32),
        query_z=block(nz, heads, cut, F32),
        query_x=block(nx, share, cut, F32),
    )
    results = dict(
        attended=((row_count, HD), BF16),
        mixed=((per * rows, width), BF16),
        dscore=((heads, per * rows), BF16),
        d_query=((heads, width), F32),
    )
    names = [*results, *buffers]
    job_sems = [job.sems() for job in jobs.values()]

    def kernel(tok, aq, av, wq, wk, wv, gn, go, *rest):
        r = SimpleNamespace(**dict(zip(names, rest)))
        refs = dict(
            tokens=(tok, r.grouped),
            scores=(r.s_own, r.s_all),
            value=(av, r.value_all),
            pooled=(r.pooled0, r.pooled1, r.pooled2, r.pooled3),
            normed=(r.normed_own, r.normed_all),
            w_query=(wq, r.weights),
            w_key=(wk, r.weights),
            w_value=(wv, r.weights),
            kv=(r.kv_own, r.kv_all),
            dkv=(r.dkv0, r.dkv1, r.dkv2, r.dkv3),
            grad=(r.grad0, r.grad1, r.grad2, r.grad3),
            d_pooled=(r.dp_own, r.dp_all),
            dmix=(r.dmix0, r.dmix1, r.dmix2, r.dmix3),
            dscore=(r.dscore_own, r.dscore_all),
            back=(r.back_b, r.mixed),
            query_z=(r.query_part, r.query_z),
            query_x=(r.query_line, r.query_x),
            query=(r.query_done, r.query_wide),
            query_all=(r.query_wide, r.d_query),
        )
        left, ready_jobs = list(rest[len(names) :]), {}
        for (name, job), wanted in zip(jobs.items(), job_sems):
            ready_jobs[name] = bound(job, left[: len(wanted)], refs[name])
            left = left[len(wanted) :]
        j = SimpleNamespace(**ready_jobs)
        ring = (j.w_key, j.w_value, j.w_query)

        def t_group(g):
            return r.grouped[:, :, g * 16 : (g + 1) * 16, :].reshape(lanes, cut)

        i = lax.axis_index(VAR)
        greeted = barrier(jobs["tokens"].peers() + jobs["value"].peers())

        local = dot(aq[...], tok[...].reshape(per * rows, width), NT) * factor
        scaled = [local[:, v * rows : (v + 1) * rows] for v in range(per)]
        top = functools.reduce(jnp.maximum, scaled).astype(BF16).astype(F32)
        r.s_own[...] = jnp.concatenate([*[jnp.exp(part - top) for part in scaled], top], axis=1).astype(BF16)
        greeted()
        j.scores.start()
        j.value.start()
        j.tokens.start()
        j.scores.middle()
        j.value.middle()

        iota = lambda shape, dim: lax.broadcasted_iota(jnp.int32, shape, dim)
        ones = lambda where: where.astype(F32).astype(BF16)
        wide_mask = lax.rem(iota((16, lanes), 1), 16) == iota((16, lanes), 0)
        tall_mask = lax.rem(iota((lanes, tall), 0), 16) == lax.rem(iota((lanes, tall), 1), 16)
        spread_heads = ones(iota((heads, tall), 1) // 16 == iota((heads, tall), 0))
        at, to = iota((tall, tall), 0), iota((tall, tall), 1)
        to_patches = ones(to == lax.rem(at, heads) * 16 + at // heads)
        to_heads = ones(to == lax.rem(at, 16) * heads + at // 16)

        j.scores.landed()
        scores = r.s_all[...].astype(F32)
        for g in range(groups):
            picked = lambda n, v: scores[n, :, v * rows + g * 16 : v * rows + (g + 1) * 16]
            over = lambda pick: jnp.concatenate([pick(n, v) for n in range(n_var) for v in range(per)], axis=1)
            tops = over(lambda n, v: picked(n, per))
            e = over(picked) * jnp.exp(tops - over_vars(jnp.maximum, tops))
            mixw = e / over_vars(jnp.add, e)
            for o in range(octets):
                r.mix[g * octets + o] = mixw[o * 8 : (o + 1) * 8]
            mix_b = mixw.astype(BF16)
            full = jnp.broadcast_to(mix_b.astype(F32)[:, None, :], (heads, 16, lanes))
            full = jnp.where(wide_mask[None], full, 0.0)
            r.mix_wide[g] = full.astype(BF16).reshape(tall, lanes)
            r.mix_tall[g] = jnp.where(tall_mask, dot(mix_b, spread_heads, TN), 0.0).astype(BF16)
        j.value.landed()
        j.scores.sent()
        j.value.sent()
        j.tokens.landed()
        for w in ring:
            w.start()

        for g in range(groups):
            r.summary[g] = dot(r.mix_wide[g], t_group(g)).astype(BF16)
        for h in range(heads):
            here = slice(h * 16, (h + 1) * 16)
            part = jnp.concatenate([r.summary[g, here, :] for g in range(groups)], axis=0)
            part = dot(part, r.value_all[h]).astype(BF16)
            for g in range(groups):
                r.stack[g, here, :] = part[g * 16 : (g + 1) * 16]
        for g in range(groups):
            part = dot(to_patches, r.stack[g]).astype(BF16)
            for n in range(at_once):
                r.pooled0[g * at_once + n] = part[n * line : (n + 1) * line]
        j.pooled.start()
        j.pooled.push()
        for w in ring:
            w.step(1)
        pooled = j.pooled.landed().astype(BF16).astype(F32).reshape(own, heads, HD)
        mean = lambda a: jnp.sum(jnp.sum(a, axis=1, keepdims=True), axis=2, keepdims=True) / width
        center = mean(pooled)
        inv_std = lax.rsqrt(mean((pooled - center) ** 2) + EPS)
        unit = (pooled - center) * inv_std
        r.normed_own[...] = (unit * gn[...][None]).astype(BF16).reshape(line, HD)
        j.normed.start()
        r.unit[...] = unit.reshape(line, HD)
        r.inv[...] = jnp.broadcast_to(inv_std, (own, heads, HD)).reshape(line, HD)
        for w in ring:
            w.step(2)
        j.normed.middle()
        for t in range(3, ny // 2 + 1):
            for w in ring:
                w.step(t)
        j.normed.landed()

        def widen(g):
            src = r.normed_all[pl.ds(g * at_once, at_once)].reshape(tall, HD)
            part = dot(to_heads, src).astype(BF16)
            for h in range(heads):
                r.wide[pl.ds(pl.multiple_of(g * 16, 16), 16), h * HD : (h + 1) * HD] = part[h * 16 : (h + 1) * 16]

        loop(0, n_seq // at_once, widen)
        j.w_key.landed()
        j.w_value.landed()
        kv_weights = r.weights[:, :, HD:].reshape(width, 2 * HD)
        r.kv_own[...] = dot(r.wide[...], kv_weights).astype(BF16)
        j.kv.start()
        j.w_query.landed()
        queries = dot(r.wide[...], r.weights[:, :, :HD].reshape(width, HD)).astype(BF16)
        j.kv.middle()
        j.kv.landed()

        keys = r.kv_all[:, :, :HD].reshape(n_var * row_count, HD)
        values = r.kv_all[:, :, HD:].reshape(n_var * row_count, HD)
        grad = go[...]
        logits = dot(queries, keys, NT) * factor
        expo = jnp.exp(logits - jnp.max(logits, axis=1, keepdims=True))
        probs = expo / jnp.sum(expo, axis=1, keepdims=True)
        probs_b = probs.astype(BF16)
        dprob = dot(grad, values, NT)
        dlogit = (probs * (dprob - jnp.sum(probs * dprob, axis=1, keepdims=True)) * factor).astype(BF16)
        r.dkv0[:, :, :HD] = dot(dlogit, queries, TN).astype(BF16).reshape(n_var, row_count, HD)
        r.dkv0[:, :, HD:] = dot(probs_b, grad, TN).astype(BF16).reshape(n_var, row_count, HD)
        j.dkv.start()
        r.attended[...] = dot(probs_b, values).astype(BF16)
        dquery = dot(dlogit, keys).astype(BF16)
        j.dkv.push()
        dkv = j.dkv.landed().astype(BF16)

        dqkv = jnp.concatenate([dquery, dkv], axis=1)
        r.wide[...] = dot(dqkv, r.weights[...].reshape(width, 3 * HD), NT).astype(BF16)

        def narrow(g):
            at = pl.ds(pl.multiple_of(g * 16, 16), 16)
            src = jnp.concatenate([r.wide[at, h * HD : (h + 1) * HD] for h in range(heads)], axis=0)
            part = dot(to_patches, src).astype(BF16)
            for n in range(at_once):
                r.grad0[g * at_once + n] = part[n * line : (n + 1) * line]

        loop(0, n_seq // at_once, narrow)
        j.grad.start()
        j.grad.push()
        scaled = j.grad.landed().reshape(own, heads, HD) * gn[...][None]
        unit = r.unit[...].reshape(own, heads, HD)
        inv_std = r.inv[...].reshape(own, heads, HD)
        d_pooled = inv_std * (scaled - mean(scaled) - unit * mean(scaled * unit))
        r.dp_own[...] = d_pooled.astype(BF16).reshape(line, HD)
        j.d_pooled.start()
        j.d_pooled.middle()
        j.d_pooled.landed()

        for g in range(groups):
            src = r.dp_all[g * at_once : (g + 1) * at_once].reshape(tall, HD)
            r.stack[g] = dot(to_heads, src).astype(BF16)
        for h in range(heads):
            here = slice(h * 16, (h + 1) * 16)
            part = jnp.concatenate([r.stack[g, here, :] for g in range(groups)], axis=0)
            part = dot(part, r.value_all[h], NT).astype(BF16)
            for g in range(groups):
                r.d_summary[g, here, :] = part[g * 16 : (g + 1) * 16]
        for g in range(groups):
            part = dot(r.mix_tall[g], r.d_summary[g]).astype(BF16).reshape(n_var, per, 16, cut)
            for v in range(per):
                r.back_b[:, v * rows + g * 16 : v * rows + (g + 1) * 16, :] = part[:, v]
        j.back.some(0, 1, 2)
        for g in range(groups):
            cross = dot(r.d_summary[g], t_group(g), NT).reshape(heads, 16, lanes)
            dmix = jnp.sum(jnp.where(wide_mask[None], cross, 0.0), axis=1)
            for o in range(octets):
                r.dmix0[g * octets + o] = dmix[o * 8 : (o + 1) * 8]
        j.dmix.start()
        j.dmix.push()
        j.back.some(3)
        dmix = j.dmix.landed()
        mixw = r.mix[i]
        dscore = mixw * (dmix - over_vars(jnp.add, mixw * dmix)) * factor
        r.dscore_own[...] = jnp.concatenate([dscore[:, : lanes // 2], dscore[:, lanes // 2 :]], axis=0).astype(BF16)
        j.dscore.start()
        j.back.some(4)
        j.dscore.middle()
        j.dscore.landed()
        j.back.some(7, 6)

        query_part = jnp.zeros((heads, cut), F32)
        mine = jnp.zeros((heads, per * rows), F32)
        lane, column = iota((lanes, per * rows), 0) - i * chunk, iota((lanes, per * rows), 1)
        for g in range(groups):
            halves = r.dscore_all[g * octets : (g + 1) * octets].astype(F32)
            dscore = jnp.concatenate([halves[:, :8], halves[:, 8:]], axis=2).reshape(heads, lanes).astype(BF16)
            query_part = query_part + dot(dscore, t_group(g))
            at_lane = column // rows * 16 + lax.rem(column, 16)
            here = (lane == at_lane) & (lax.rem(column, rows) // 16 == g)
            mine = mine + dot(dscore, ones(here))
        r.query_part[...] = query_part
        j.query_z.start()
        r.dscore[...] = mine.astype(BF16)
        j.query_z.landed()
        r.query_line[...] = jnp.sum(r.query_z[...], axis=0)
        j.query_x.start()
        j.query_x.landed()
        r.query_done[...] = jnp.sum(r.query_x[...], axis=0)
        j.query.start()
        j.back.some(8, 5)
        j.query.middle()
        for job in (j.tokens, j.pooled, j.normed, *ring, j.kv, j.dkv, j.grad, j.d_pooled, j.dmix, j.dscore):
            job.sent()
        j.query.landed()
        j.query_all.start()
        j.query_z.sent()
        j.query_x.sent()
        j.query.sent()
        j.query_all.landed()
        j.query_all.sent()
        j.back.landed()
        j.back.sent()

    in_vmem = pl.BlockSpec(memory_space=pltpu.VMEM)
    return pl.pallas_call(
        kernel,
        name="encoder",
        out_shape=[jax.ShapeDtypeStruct(*results[name]) for name in results],
        in_specs=[in_vmem] * 8,
        out_specs=[in_vmem] * len(results),
        scratch_shapes=[pltpu.VMEM(*buffers[name]) for name in buffers]
        + [sem for wanted in job_sems for sem in wanted],
        compiler_params=pltpu.CompilerParams(
            collective_id=0, has_side_effects=True, vmem_limit_bytes=60 * 1024 * 1024
        ),
    )(tokens, agg_query, agg_value, w_query, w_key, w_value, gain, grad_out)


def per_device(n_var, n_seq, tokens, agg_query, agg_value, w_query, w_key, w_value, gain, d_out):
    heads = agg_query.shape[0]
    attended, mixed, dscore, d_query = program(
        n_var, n_seq, tokens, agg_query, agg_value, w_query, w_key, w_value,
        gain.reshape(heads, HD), d_out.reshape(-1, HD),
    )
    d_tokens = (mixed.astype(F32) + dot(dscore, agg_query, TN)).astype(BF16).reshape(tokens.shape)
    return (attended.reshape(d_out.shape), d_tokens, d_query)


def solution(mesh):
    return jax.shard_map(
        functools.partial(per_device, mesh.shape[VAR], mesh.shape[SEQ]),
        mesh=mesh,
        in_specs=(
            P(VAR, SEQ, None),
            P(),
            P(VAR, SEQ),
            P(VAR, SEQ),
            P(VAR, SEQ),
            P(VAR, SEQ),
            P(),
            P(None, VAR, SEQ),
        ),
        out_specs=(P(None, VAR, SEQ), P(VAR, SEQ, None), P()),
        check_vma=False,
    )
```

```python
import functools
from types import SimpleNamespace

import jax
import jax.numpy as jnp
from jax import lax
from jax.experimental import pallas as pl
from jax.experimental.pallas import tpu as pltpu
from jax.sharding import PartitionSpec as P

HD = 128
EPS = 1e-05
NZ = 8
MESH = pl.DeviceIdType.MESH
F32 = jnp.float32
BF16 = jnp.bfloat16
VAR, SEQ = "var", "seq"
X, Z = "x", "z"
NT = ((1,), (1,))
TN = ((0,), (0,))


def remote(src, dst, send, recv, device):
    return pltpu.make_async_remote_copy(
        src_ref=src, dst_ref=dst, send_sem=send, recv_sem=recv, device_id=device, device_id_type=MESH
    )


def loop(first, last, body):
    def step(k, carry):
        body(k)
        return carry

    lax.fori_loop(first, last, step, 0)


def slot(ref, j):
    return ref.at[j]


def whole(ref, j):
    return ref


def dma(*shape):
    return pltpu.SemaphoreType.DMA(shape)


def first_blocks(ref, n):
    return ref.at[pl.ds(0, n)]


def arrived(ref, sem):
    remote(ref, ref, sem, sem, {}).wait_recv()


def left(ref, sem):
    remote(ref, ref, sem, sem, {}).wait_send()


class Direct:
    def __init__(self, axis, n, src=slot, dst=slot, blocks=first_blocks):
        self.axis, self.n, self.src, self.dst, self.blocks = axis, n, src, dst, blocks

    def sems(self):
        return [dma(), dma(), dma()]

    def here(self):
        if self.axis == VAR:
            return lax.axis_index(VAR)
        return lax.axis_index(SEQ) // NZ if self.axis == X else lax.rem(lax.axis_index(SEQ), NZ)

    def device(self, to):
        if self.axis == VAR:
            return {VAR: to}
        me = lax.axis_index(SEQ)
        return {SEQ: to * NZ + lax.rem(me, NZ) if self.axis == X else me // NZ * NZ + to}

    def peers(self):
        return [(self.n - 1, lambda k: self.device(lax.rem(self.here() + k + 1, self.n)))]

    def send(self, x, o, sems, k):
        me = self.here()
        to = lax.rem(me + k, self.n)
        remote(self.src(x, to), self.dst(o, me), sems[0], sems[1], self.device(to)).start()

    def own(self, x, o, sems):
        me = self.here()
        return pltpu.make_async_copy(self.src(x, me), self.dst(o, me), sems[2])

    def start(self, x, o, sems):
        loop(1, self.n, lambda k: self.send(x, o, sems, k))
        self.own(x, o, sems).start()

    def some(self, x, o, sems, *offsets):
        for k in offsets:
            if k == 0:
                self.own(x, o, sems).start()
            else:
                self.send(x, o, sems, k)
                if 2 * k != self.n:
                    self.send(x, o, sems, self.n - k)

    def landed(self, x, o, sems):
        self.own(x, o, sems).wait()
        arrived(self.blocks(o, self.n - 1), sems[1])

    def sent(self, x, o, sems):
        left(self.blocks(o, self.n - 1), sems[0])


class GatherSeq:
    def __init__(self, n):
        self.nz = NZ
        self.nx = n // NZ

    def sems(self):
        return [dma(), dma(self.nz), dma(), dma(self.nx), dma()]

    def place(self):
        me = lax.axis_index(SEQ)
        return me, me // self.nz, lax.rem(me, self.nz)

    def peers(self):
        me, x, z = self.place()
        return [
            (self.nz - 1, lambda k: {SEQ: x * self.nz + lax.rem(z + k + 1, self.nz)}),
            (self.nx - 1, lambda k: {SEQ: lax.rem(x + k + 1, self.nx) * self.nz + z}),
        ]

    def along_z(self, a, o, sems, k, received):
        me, x, z = self.place()
        at = lax.rem(z + self.nz - k, self.nz) if received else z
        return remote(
            a, o.at[x * self.nz + at], sems[0], sems[1].at[k],
            {SEQ: x * self.nz + lax.rem(z + k, self.nz)},
        )

    def along_x(self, a, o, sems, k, m):
        me, x, z = self.place()
        at = x * self.nz + lax.rem(z + self.nz - k, self.nz)
        src = a if isinstance(k, int) and k == 0 else o.at[at]
        to = lax.rem(x + m, self.nx) * self.nz + z
        remote(src, o.at[at], sems[2], sems[3].at[m], {SEQ: to}).start()

    def own(self, a, o, sems):
        return pltpu.make_async_copy(a, o.at[lax.axis_index(SEQ)], sems[4])

    def start(self, a, o, sems):
        loop(1, self.nz, lambda k: self.along_z(a, o, sems, k, False).start())
        loop(1, self.nx, lambda m: self.along_x(a, o, sems, 0, m))
        self.own(a, o, sems).start()

    def middle(self, a, o, sems):
        def forward(k):
            self.along_z(a, o, sems, k, True).wait_recv()
            loop(1, self.nx, lambda m: self.along_x(a, o, sems, k, m))

        loop(1, self.nz, forward)

    def landed(self, a, o, sems):
        self.own(a, o, sems).wait()
        loop(1, self.nx, lambda m: arrived(first_blocks(o, self.nz), sems[3].at[m]))

    def sent(self, a, o, sems):
        left(first_blocks(o, self.nz - 1), sems[0])
        left(first_blocks(o, self.nz * (self.nx - 1)), sems[2])


class GatherVar:
    def __init__(self, n, dst=slot, blocks=first_blocks):
        self.n, self.ny, self.dst, self.blocks = n, n // 2, dst, blocks

    def sems(self):
        return [dma(), dma(self.ny), dma(), dma(), dma()]

    def place(self):
        me = lax.axis_index(VAR)
        return me, me // 2, lax.rem(me, 2)

    def far(self, src, o, sems, block, way, k):
        me, y, c = self.place()
        at = 2 * lax.rem(y + self.ny - block, self.ny) + c
        src = self.dst(o, at) if src is None else src
        return remote(
            src, self.dst(o, at), sems[0], sems[1].at[k], {VAR: 2 * lax.rem(y + way, self.ny) + c}
        )

    def arrived(self, a, o, sems, k):
        me, y, c = self.place()
        arrived(self.dst(o, 2 * lax.rem(y + self.ny - k, self.ny) + c), sems[1].at[k])

    def across(self, o, sems, k, first=None):
        me, y, c = self.place()
        at = self.dst(o, 2 * lax.rem(y + self.ny - k, self.ny) + c)
        remote(at if first is None else first, at, sems[2], sems[3], {VAR: 2 * y + 1 - c}).start()

    def own(self, a, o, sems):
        return pltpu.make_async_copy(a, self.dst(o, lax.axis_index(VAR)), sems[4])

    def begin(self, a, o, sems):
        loop(1, self.ny, lambda k: self.far(a, o, sems, 0, k, k).start())

    def start(self, a, o, sems):
        self.begin(a, o, sems)
        self.across(o, sems, 0, a)
        self.own(a, o, sems).start()

    def middle(self, a, o, sems):
        def forward(k):
            self.arrived(a, o, sems, k)
            self.across(o, sems, k)

        loop(1, self.ny, forward)

    def landed(self, a, o, sems):
        self.own(a, o, sems).wait()
        arrived(self.blocks(o, self.ny), sems[3])

    def sent(self, a, o, sems):
        left(self.blocks(o, self.ny - 1), sems[0])
        left(self.blocks(o, self.ny), sems[2])


class RingVar(GatherVar):
    def begin(self, a, o, sems):
        self.far(a, o, sems, 0, 1, 1).start()
        self.far(a, o, sems, 0, self.ny - 1, self.ny - 1).start()

    def step(self, a, o, sems, t):
        half = self.ny // 2
        self.arrived(a, o, sems, t)
        if t < half:
            self.far(None, o, sems, t, 1, t + 1).start()
        self.across(o, sems, t)
        if t < half:
            self.arrived(a, o, sems, self.ny - t)
            if t < half - 1:
                self.far(None, o, sems, self.ny - t, self.ny - 1, self.ny - t - 1).start()
            self.across(o, sems, self.ny - t)


class TwoStepVar(GatherVar):
    def begin(self, a, o, sems):
        for k in (2, 6, 1, 7):
            self.far(a, o, sems, 0, k, k).start()

    def opposite(self, o, sems):
        me, y, c = self.place()
        return self.far(None, o, sems, 2 + 4 * c, 2 + 4 * c, 4)

    def middle(self, a, o, sems):
        me, y, c = self.place()
        self.arrived(a, o, sems, 2)
        self.arrived(a, o, sems, 6)
        self.opposite(o, sems).start()
        self.far(None, o, sems, 2, 1, 3).start()
        self.far(None, o, sems, 6, 7, 5).start()
        for k in (2, 6):
            self.across(o, sems, k)
        for k in (1, 7, 3, 5, 4):
            self.arrived(a, o, sems, k)
            self.across(o, sems, k)


class ReduceVar:
    def __init__(self, n):
        self.n, self.ny = n, n // 2

    def sems(self):
        return [dma(), dma(self.ny), dma(), dma()]

    def place(self):
        me = lax.axis_index(VAR)
        return me // 2, lax.rem(me, 2)

    def across(self, b, held, sems, k):
        y, c = self.place()
        yy = lax.rem(y + k + 1, self.ny)
        return remote(b.at[2 * yy + 1 - c], held.at[yy], sems[0], sems[1].at[k], {VAR: 2 * y + 1 - c})

    def along_y(self, summed, landed, sems, k):
        y, c = self.place()
        yy = lax.rem(y + k + 1, self.ny)
        remote(summed.at[yy], landed.at[y], sems[2], sems[3], {VAR: 2 * yy + c}).start()

    def start(self, b, held, summed, landed, sems):
        loop(0, self.ny, lambda k: self.across(b, held, sems, k).start())

    def push(self, b, held, summed, landed, sems):
        y, c = self.place()

        def add(k):
            yy = lax.rem(y + k + 1, self.ny)
            self.across(b, held, sems, k).wait_recv()
            total = b[2 * yy + c].astype(F32) + held[yy].astype(F32)
            summed[yy] = total.astype(summed.dtype)

        def step(k):
            add(k)
            self.along_y(summed, landed, sems, k)

        loop(0, self.ny - 1, step)
        add(self.ny - 1)

    def landed(self, b, held, summed, landed, sems):
        y, c = self.place()
        total = summed[y].astype(F32)
        arrived(first_blocks(landed, self.ny - 1), sems[3])
        for k in range(self.ny - 1):
            total = total + landed[lax.rem(y + self.ny - k - 1, self.ny)].astype(F32)
        return total

    def sent(self, b, held, summed, landed, sems):
        left(first_blocks(b, self.ny), sems[0])
        left(first_blocks(landed, self.ny - 1), sems[2])


class ReduceSeq:
    def __init__(self, n):
        self.nz, self.nx = NZ, n // NZ

    def sems(self):
        return [dma(), dma(self.nz), dma(), dma()]

    def place(self):
        me = lax.axis_index(SEQ)
        return me // self.nz, lax.rem(me, self.nz)

    def along_x(self, b, held, sems, k, m):
        x, z = self.place()
        zz = lax.rem(z + k + 1, self.nz)
        to = lax.rem(x + m, self.nx)
        remote(
            b.at[to * self.nz + zz], held.at[x * self.nz + zz], sems[0], sems[1].at[k], {SEQ: to * self.nz + z}
        ).start()

    def along_z(self, summed, landed, sems, k):
        x, z = self.place()
        zz = lax.rem(z + k + 1, self.nz)
        remote(summed.at[zz], landed.at[z], sems[2], sems[3], {SEQ: x * self.nz + zz}).start()

    def start(self, b, held, summed, landed, sems):
        def send(k):
            loop(1, self.nx, lambda m: self.along_x(b, held, sems, k, m))

        loop(0, self.nz, send)

    def push(self, b, held, summed, landed, sems):
        x, z = self.place()

        def add(k):
            zz = lax.rem(z + k + 1, self.nz)
            total = b[x * self.nz + zz].astype(F32)
            arrived(first_blocks(held, self.nx - 1), sems[1].at[k])
            for m in range(1, self.nx):
                total = total + held[lax.rem(x + self.nx - m, self.nx) * self.nz + zz].astype(F32)
            summed[zz] = total.astype(summed.dtype)

        def step(k):
            add(k)
            self.along_z(summed, landed, sems, k)

        loop(0, self.nz - 1, step)
        add(self.nz - 1)

    def landed(self, b, held, summed, landed, sems):
        x, z = self.place()
        total = summed[z].astype(F32)
        arrived(first_blocks(landed, self.nz - 1), sems[3])
        for k in range(self.nz - 1):
            total = total + landed[lax.rem(z + self.nz - k - 1, self.nz)].astype(F32)
        return total

    def sent(self, b, held, summed, landed, sems):
        left(first_blocks(b, self.nz * (self.nx - 1)), sems[0])
        left(first_blocks(landed, self.nz - 1), sems[2])


def bound(job, sems, refs):
    def fill(phase):
        return lambda *more: phase(*refs, sems, *more)

    return SimpleNamespace(
        **{name: fill(getattr(job, name)) for name in dir(job) if not name.startswith("_") and name != "n"
           and callable(getattr(job, name))}
    )


def barrier(groups):
    sem = pltpu.get_barrier_semaphore()
    for count, to in groups:
        loop(0, count, lambda k: pl.semaphore_signal(sem, inc=1, device_id=to(k), device_id_type=MESH))
    return lambda: pl.semaphore_wait(sem, sum(count for count, _ in groups))


def dot(a, b, dims=((1,), (0,))):
    return lax.dot_general(a, b, (dims, ((), ())), preferred_element_type=F32)


def over_vars(fold, z):
    out = z[:, :128]
    for at in range(128, z.shape[1], 128):
        out = fold(out, z[:, at : at + 128])
    for shift in (64, 32, 16):
        out = fold(out, pltpu.roll(out, shift, 1))
    return jnp.concatenate([out] * (z.shape[1] // 128), axis=1)


def program(n_var, n_seq, tokens, agg_query, agg_value, w_query, w_key, w_value, gain, grad_out):
    factor = HD ** (-0.5)
    per, rows, width = tokens.shape
    heads = agg_query.shape[0]
    octets = heads // 8
    cut = width // n_var
    own = rows // n_var
    line = own * heads
    groups = rows // 16
    chunk = per * 16
    lanes = n_var * chunk
    tall = 16 * heads
    row_count = n_seq * own
    at_once = 16 // own
    ny, nz, nx = n_var // 2, NZ, n_seq // NZ
    share = heads // nx

    at_cut = lambda j: pl.ds(pl.multiple_of(j * cut, cut), cut)
    few = lambda j: pl.ds(pl.multiple_of(j * share, share), share)
    weight = lambda w: RingVar(
        n_var, lambda o, j: o.at[j, :, pl.ds(w * HD, HD)], lambda o, n: o.at[pl.ds(0, n), :, pl.ds(w * HD, HD)]
    )
    jobs = dict(
        tokens=Direct(VAR, n_var, lambda x, j: x.at[:, :, at_cut(j)], slot),
        scores=GatherVar(n_var),
        value=GatherSeq(n_seq),
        pooled=ReduceVar(n_var),
        normed=GatherSeq(n_seq),
        w_query=weight(0),
        w_key=weight(1),
        w_value=weight(2),
        kv=TwoStepVar(n_var),
        dkv=ReduceVar(n_var),
        grad=ReduceSeq(n_seq),
        d_pooled=GatherVar(n_var),
        dmix=ReduceVar(n_var),
        dscore=GatherVar(n_var),
        back=Direct(VAR, n_var, slot, lambda o, j: o.at[:, at_cut(j)], lambda o, n: o.at[:, pl.ds(0, n * cut)]),
        query_z=Direct(Z, nz, whole),
        query_x=Direct(X, nx, lambda x, j: x.at[few(j)]),
        query=GatherVar(n_var, lambda o, j: o.at[:, at_cut(j)], lambda o, n: o.at[:, pl.ds(0, n * cut)]),
        query_all=Direct(X, nx, whole, lambda o, j: o.at[few(j)], lambda o, n: o.at[pl.ds(0, n * share)]),
    )

    block = lambda n, r=line, c=HD, t=BF16: ((n, r, c), t)

    def through(blocks, *rest):
        return block(blocks, *rest), block(ny, *rest), block(ny, *rest), block(ny, *rest)

    pooled, dkv = through(n_var), through(n_var, row_count, 2 * HD)
    dmix = through(n_var, 8, lanes, F32)
    buffers = dict(
        grouped=((n_var, per, rows, cut), BF16),
        s_own=((heads, (per + 1) * rows), BF16),
        s_all=block(n_var, heads, (per + 1) * rows),
        value_all=block(n_seq, cut, HD),
        mix=block(n_var, 8, lanes, F32),
        mix_wide=block(groups, tall, lanes),
        mix_tall=block(groups, lanes, tall),
        summary=block(groups, tall, cut),
        stack=block(groups, tall, HD),
        pooled0=pooled[0], pooled1=pooled[1], pooled2=pooled[2], pooled3=pooled[3],
        unit=((line, HD), F32),
        inv=((line, HD), F32),
        normed_own=((line, HD), BF16),
        normed_all=block(n_seq),
        weights=block(n_var, cut, 3 * HD),
        wide=((row_count, width), BF16),
        kv_own=((row_count, 2 * HD), BF16),
        kv_all=block(n_var, row_count, 2 * HD),
        dkv0=dkv[0], dkv1=dkv[1], dkv2=dkv[2], dkv3=dkv[3],
        grad0=block(n_seq), grad1=block(n_seq), grad2=block(nz), grad3=block(nz),
        dp_own=((line, HD), BF16),
        dp_all=block(n_var),
        d_summary=block(groups, tall, cut),
        dmix0=dmix[0], dmix1=dmix[1], dmix2=dmix[2], dmix3=dmix[3],
        dscore_own=((16, lanes // 2), BF16),
        dscore_all=block(n_var, 16, lanes // 2),
        back_b=block(n_var, per * rows, cut),
        query_part=((heads, cut), F32),
        query_line=((heads, cut), F32),
        query_done=((share, cut), F32),
        query_wide=((share, width), F32),
        query_z=block(nz, heads, cut, F32),
        query_x=block(nx, share, cut, F32),
    )
    results = dict(
        attended=((row_count, HD), BF16),
        mixed=((per * rows, width), BF16),
        dscore=((heads, per * rows), BF16),
        d_query=((heads, width), F32),
    )
    names = [*results, *buffers]
    job_sems = [job.sems() for job in jobs.values()]

    def kernel(tok, aq, av, wq, wk, wv, gn, go, *rest):
        r = SimpleNamespace(**dict(zip(names, rest)))
        refs = dict(
            tokens=(tok, r.grouped),
            scores=(r.s_own, r.s_all),
            value=(av, r.value_all),
            pooled=(r.pooled0, r.pooled1, r.pooled2, r.pooled3),
            normed=(r.normed_own, r.normed_all),
            w_query=(wq, r.weights),
            w_key=(wk, r.weights),
            w_value=(wv, r.weights),
            kv=(r.kv_own, r.kv_all),
            dkv=(r.dkv0, r.dkv1, r.dkv2, r.dkv3),
            grad=(r.grad0, r.grad1, r.grad2, r.grad3),
            d_pooled=(r.dp_own, r.dp_all),
            dmix=(r.dmix0, r.dmix1, r.dmix2, r.dmix3),
            dscore=(r.dscore_own, r.dscore_all),
            back=(r.back_b, r.mixed),
            query_z=(r.query_part, r.query_z),
            query_x=(r.query_line, r.query_x),
            query=(r.query_done, r.query_wide),
            query_all=(r.query_wide, r.d_query),
        )
        left, ready_jobs = list(rest[len(names) :]), {}
        for (name, job), wanted in zip(jobs.items(), job_sems):
            ready_jobs[name] = bound(job, left[: len(wanted)], refs[name])
            left = left[len(wanted) :]
        j = SimpleNamespace(**ready_jobs)
        ring = (j.w_key, j.w_value, j.w_query)

        def t_group(g):
            return r.grouped[:, :, g * 16 : (g + 1) * 16, :].reshape(lanes, cut)

        i = lax.axis_index(VAR)
        greeted = barrier(jobs["tokens"].peers() + jobs["value"].peers())

        local = dot(aq[...], tok[...].reshape(per * rows, width), NT) * factor
        scaled = [local[:, v * rows : (v + 1) * rows] for v in range(per)]
        top = functools.reduce(jnp.maximum, scaled).astype(BF16).astype(F32)
        r.s_own[...] = jnp.concatenate([*[jnp.exp(part - top) for part in scaled], top], axis=1).astype(BF16)
        greeted()
        j.scores.start()
        j.value.start()
        j.tokens.start()
        for w in ring:
            w.start()
        j.scores.middle()
        j.value.middle()

        iota = lambda shape, dim: lax.broadcasted_iota(jnp.int32, shape, dim)
        ones = lambda where: where.astype(F32).astype(BF16)
        wide_mask = lax.rem(iota((16, lanes), 1), 16) == iota((16, lanes), 0)
        tall_mask = lax.rem(iota((lanes, tall), 0), 16) == lax.rem(iota((lanes, tall), 1), 16)
        spread_heads = ones(iota((heads, tall), 1) // 16 == iota((heads, tall), 0))
        at, to = iota((tall, tall), 0), iota((tall, tall), 1)
        to_patches = ones(to == lax.rem(at, heads) * 16 + at // heads)
        to_heads = ones(to == lax.rem(at, 16) * heads + at // 16)

        j.scores.landed()
        scores = r.s_all[...].astype(F32)
        for g in range(groups):
            picked = lambda n, v: scores[n, :, v * rows + g * 16 : v * rows + (g + 1) * 16]
            over = lambda pick: jnp.concatenate([pick(n, v) for n in range(n_var) for v in range(per)], axis=1)
            tops = over(lambda n, v: picked(n, per))
            e = over(picked) * jnp.exp(tops - over_vars(jnp.maximum, tops))
            mixw = e / over_vars(jnp.add, e)
            for o in range(octets):
                r.mix[g * octets + o] = mixw[o * 8 : (o + 1) * 8]
            mix_b = mixw.astype(BF16)
            full = jnp.broadcast_to(mix_b.astype(F32)[:, None, :], (heads, 16, lanes))
            full = jnp.where(wide_mask[None], full, 0.0)
            r.mix_wide[g] = full.astype(BF16).reshape(tall, lanes)
            r.mix_tall[g] = jnp.where(tall_mask, dot(mix_b, spread_heads, TN), 0.0).astype(BF16)
        j.value.landed()
        j.scores.sent()
        j.value.sent()
        j.tokens.landed()

        for g in range(groups):
            r.summary[g] = dot(r.mix_wide[g], t_group(g)).astype(BF16)
        for h in range(heads):
            here = slice(h * 16, (h + 1) * 16)
            part = jnp.concatenate([r.summary[g, here, :] for g in range(groups)], axis=0)
            part = dot(part, r.value_all[h]).astype(BF16)
            for g in range(groups):
                r.stack[g, here, :] = part[g * 16 : (g + 1) * 16]
        for g in range(groups):
            part = dot(to_patches, r.stack[g]).astype(BF16)
            for n in range(at_once):
                r.pooled0[g * at_once + n] = part[n * line : (n + 1) * line]
        j.pooled.start()
        j.pooled.push()
        for w in ring:
            w.step(1)
        pooled = j.pooled.landed().astype(BF16).astype(F32).reshape(own, heads, HD)
        mean = lambda a: jnp.sum(jnp.sum(a, axis=1, keepdims=True), axis=2, keepdims=True) / width
        center = mean(pooled)
        inv_std = lax.rsqrt(mean((pooled - center) ** 2) + EPS)
        unit = (pooled - center) * inv_std
        r.normed_own[...] = (unit * gn[...][None]).astype(BF16).reshape(line, HD)
        j.normed.start()
        r.unit[...] = unit.reshape(line, HD)
        r.inv[...] = jnp.broadcast_to(inv_std, (own, heads, HD)).reshape(line, HD)
        for w in ring:
            w.step(2)
        j.normed.middle()
        for t in range(3, ny // 2 + 1):
            for w in ring:
                w.step(t)
        j.normed.landed()

        def widen(g):
            src = r.normed_all[pl.ds(g * at_once, at_once)].reshape(tall, HD)
            part = dot(to_heads, src).astype(BF16)
            for h in range(heads):
                r.wide[pl.ds(pl.multiple_of(g * 16, 16), 16), h * HD : (h + 1) * HD] = part[h * 16 : (h + 1) * 16]

        loop(0, n_seq // at_once, widen)
        j.w_key.landed()
        j.w_value.landed()
        kv_weights = r.weights[:, :, HD:].reshape(width, 2 * HD)
        r.kv_own[...] = dot(r.wide[...], kv_weights).astype(BF16)
        j.kv.start()
        j.w_query.landed()
        queries = dot(r.wide[...], r.weights[:, :, :HD].reshape(width, HD)).astype(BF16)
        j.kv.middle()
        j.kv.landed()

        keys = r.kv_all[:, :, :HD].reshape(n_var * row_count, HD)
        values = r.kv_all[:, :, HD:].reshape(n_var * row_count, HD)
        grad = go[...]
        logits = dot(queries, keys, NT) * factor
        expo = jnp.exp(logits - jnp.max(logits, axis=1, keepdims=True))
        probs = expo / jnp.sum(expo, axis=1, keepdims=True)
        probs_b = probs.astype(BF16)
        dprob = dot(grad, values, NT)
        dlogit = (probs * (dprob - jnp.sum(probs * dprob, axis=1, keepdims=True)) * factor).astype(BF16)
        r.dkv0[:, :, :HD] = dot(dlogit, queries, TN).astype(BF16).reshape(n_var, row_count, HD)
        r.dkv0[:, :, HD:] = dot(probs_b, grad, TN).astype(BF16).reshape(n_var, row_count, HD)
        j.dkv.start()
        r.attended[...] = dot(probs_b, values).astype(BF16)
        dquery = dot(dlogit, keys).astype(BF16)
        j.dkv.push()
        dkv = j.dkv.landed().astype(BF16)

        dqkv = jnp.concatenate([dquery, dkv], axis=1)
        r.wide[...] = dot(dqkv, r.weights[...].reshape(width, 3 * HD), NT).astype(BF16)

        def narrow(g):
            at = pl.ds(pl.multiple_of(g * 16, 16), 16)
            src = jnp.concatenate([r.wide[at, h * HD : (h + 1) * HD] for h in range(heads)], axis=0)
            part = dot(to_patches, src).astype(BF16)
            for n in range(at_once):
                r.grad0[g * at_once + n] = part[n * line : (n + 1) * line]

        loop(0, n_seq // at_once, narrow)
        j.grad.start()
        j.grad.push()
        scaled = j.grad.landed().reshape(own, heads, HD) * gn[...][None]
        unit = r.unit[...].reshape(own, heads, HD)
        inv_std = r.inv[...].reshape(own, heads, HD)
        d_pooled = inv_std * (scaled - mean(scaled) - unit * mean(scaled * unit))
        r.dp_own[...] = d_pooled.astype(BF16).reshape(line, HD)
        j.d_pooled.start()
        j.d_pooled.middle()
        j.d_pooled.landed()

        for g in range(groups):
            src = r.dp_all[g * at_once : (g + 1) * at_once].reshape(tall, HD)
            r.stack[g] = dot(to_heads, src).astype(BF16)
        for h in range(heads):
            here = slice(h * 16, (h + 1) * 16)
            part = jnp.concatenate([r.stack[g, here, :] for g in range(groups)], axis=0)
            part = dot(part, r.value_all[h], NT).astype(BF16)
            for g in range(groups):
                r.d_summary[g, here, :] = part[g * 16 : (g + 1) * 16]
        for g in range(groups):
            part = dot(r.mix_tall[g], r.d_summary[g]).astype(BF16).reshape(n_var, per, 16, cut)
            for v in range(per):
                r.back_b[:, v * rows + g * 16 : v * rows + (g + 1) * 16, :] = part[:, v]
        j.back.some(0, 1, 2)
        for g in range(groups):
            cross = dot(r.d_summary[g], t_group(g), NT).reshape(heads, 16, lanes)
            dmix = jnp.sum(jnp.where(wide_mask[None], cross, 0.0), axis=1)
            for o in range(octets):
                r.dmix0[g * octets + o] = dmix[o * 8 : (o + 1) * 8]
        j.dmix.start()
        j.dmix.push()
        j.back.some(3)
        dmix = j.dmix.landed()
        mixw = r.mix[i]
        dscore = mixw * (dmix - over_vars(jnp.add, mixw * dmix)) * factor
        r.dscore_own[...] = jnp.concatenate([dscore[:, : lanes // 2], dscore[:, lanes // 2 :]], axis=0).astype(BF16)
        j.dscore.start()
        j.back.some(4)
        j.dscore.middle()
        j.dscore.landed()
        j.back.some(7, 6)

        query_part = jnp.zeros((heads, cut), F32)
        mine = jnp.zeros((heads, per * rows), F32)
        lane, column = iota((lanes, per * rows), 0) - i * chunk, iota((lanes, per * rows), 1)
        for g in range(groups):
            halves = r.dscore_all[g * octets : (g + 1) * octets].astype(F32)
            dscore = jnp.concatenate([halves[:, :8], halves[:, 8:]], axis=2).reshape(heads, lanes).astype(BF16)
            query_part = query_part + dot(dscore, t_group(g))
            at_lane = column // rows * 16 + lax.rem(column, 16)
            here = (lane == at_lane) & (lax.rem(column, rows) // 16 == g)
            mine = mine + dot(dscore, ones(here))
        r.query_part[...] = query_part
        j.query_z.start()
        r.dscore[...] = mine.astype(BF16)
        j.query_z.landed()
        r.query_line[...] = jnp.sum(r.query_z[...], axis=0)
        j.query_x.start()
        j.query_x.landed()
        r.query_done[...] = jnp.sum(r.query_x[...], axis=0)
        j.query.start()
        j.back.some(8, 5)
        j.query.middle()
        for job in (j.tokens, j.pooled, j.normed, *ring, j.kv, j.dkv, j.grad, j.d_pooled, j.dmix, j.dscore):
            job.sent()
        j.query.landed()
        j.query_all.start()
        j.query_z.sent()
        j.query_x.sent()
        j.query.sent()
        j.query_all.landed()
        j.query_all.sent()
        j.back.landed()
        j.back.sent()

    in_vmem = pl.BlockSpec(memory_space=pltpu.VMEM)
    return pl.pallas_call(
        kernel,
        name="encoder",
        out_shape=[jax.ShapeDtypeStruct(*results[name]) for name in results],
        in_specs=[in_vmem] * 8,
        out_specs=[in_vmem] * len(results),
        scratch_shapes=[pltpu.VMEM(*buffers[name]) for name in buffers]
        + [sem for wanted in job_sems for sem in wanted],
        compiler_params=pltpu.CompilerParams(
            collective_id=0, has_side_effects=True, vmem_limit_bytes=60 * 1024 * 1024
        ),
    )(tokens, agg_query, agg_value, w_query, w_key, w_value, gain, grad_out)


def per_device(n_var, n_seq, tokens, agg_query, agg_value, w_query, w_key, w_value, gain, d_out):
    heads = agg_query.shape[0]
    attended, mixed, dscore, d_query = program(
        n_var, n_seq, tokens, agg_query, agg_value, w_query, w_key, w_value,
        gain.reshape(heads, HD), d_out.reshape(-1, HD),
    )
    d_tokens = (mixed.astype(F32) + dot(dscore, agg_query, TN)).astype(BF16).reshape(tokens.shape)
    return (attended.reshape(d_out.shape), d_tokens, d_query)


def solution(mesh):
    return jax.shard_map(
        functools.partial(per_device, mesh.shape[VAR], mesh.shape[SEQ]),
        mesh=mesh,
        in_specs=(
            P(VAR, SEQ, None),
            P(),
            P(VAR, SEQ),
            P(VAR, SEQ),
            P(VAR, SEQ),
            P(VAR, SEQ),
            P(),
            P(None, VAR, SEQ),
        ),
        out_specs=(P(None, VAR, SEQ), P(VAR, SEQ, None), P()),
        check_vma=False,
    )
```

```python
import functools
from types import SimpleNamespace

import jax
import jax.numpy as jnp
from jax import lax
from jax.experimental import pallas as pl
from jax.experimental.pallas import tpu as pltpu
from jax.sharding import PartitionSpec as P

HD = 128
EPS = 1e-05
NZ = 8
MESH = pl.DeviceIdType.MESH
F32 = jnp.float32
BF16 = jnp.bfloat16
VAR, SEQ = "var", "seq"
X, Z = "x", "z"
NT = ((1,), (1,))
TN = ((0,), (0,))


def remote(src, dst, send, recv, device):
    return pltpu.make_async_remote_copy(
        src_ref=src, dst_ref=dst, send_sem=send, recv_sem=recv, device_id=device, device_id_type=MESH
    )


def loop(first, last, body):
    def step(k, carry):
        body(k)
        return carry

    lax.fori_loop(first, last, step, 0)


def slot(ref, j):
    return ref.at[j]


def whole(ref, j):
    return ref


def dma(*shape):
    return pltpu.SemaphoreType.DMA(shape)


def first_blocks(ref, n):
    return ref.at[pl.ds(0, n)]


def arrived(ref, sem):
    remote(ref, ref, sem, sem, {}).wait_recv()


def left(ref, sem):
    remote(ref, ref, sem, sem, {}).wait_send()


class Direct:
    def __init__(self, axis, n, src=slot, dst=slot, blocks=first_blocks):
        self.axis, self.n, self.src, self.dst, self.blocks = axis, n, src, dst, blocks

    def sems(self):
        return [dma(), dma(), dma()]

    def here(self):
        if self.axis == VAR:
            return lax.axis_index(VAR)
        return lax.axis_index(SEQ) // NZ if self.axis == X else lax.rem(lax.axis_index(SEQ), NZ)

    def device(self, to):
        if self.axis == VAR:
            return {VAR: to}
        me = lax.axis_index(SEQ)
        return {SEQ: to * NZ + lax.rem(me, NZ) if self.axis == X else me // NZ * NZ + to}

    def peers(self):
        return [(self.n - 1, lambda k: self.device(lax.rem(self.here() + k + 1, self.n)))]

    def send(self, x, o, sems, k):
        me = self.here()
        to = lax.rem(me + k, self.n)
        remote(self.src(x, to), self.dst(o, me), sems[0], sems[1], self.device(to)).start()

    def own(self, x, o, sems):
        me = self.here()
        return pltpu.make_async_copy(self.src(x, me), self.dst(o, me), sems[2])

    def start(self, x, o, sems):
        loop(1, self.n, lambda k: self.send(x, o, sems, k))
        self.own(x, o, sems).start()

    def some(self, x, o, sems, *offsets):
        for k in offsets:
            if k == 0:
                self.own(x, o, sems).start()
            else:
                self.send(x, o, sems, k)
                if 2 * k != self.n:
                    self.send(x, o, sems, self.n - k)

    def landed(self, x, o, sems):
        self.own(x, o, sems).wait()
        arrived(self.blocks(o, self.n - 1), sems[1])

    def sent(self, x, o, sems):
        left(self.blocks(o, self.n - 1), sems[0])


class GatherSeq:
    def __init__(self, n):
        self.nz = NZ
        self.nx = n // NZ

    def sems(self):
        return [dma(), dma(self.nz), dma(), dma(self.nx), dma()]

    def place(self):
        me = lax.axis_index(SEQ)
        return me, me // self.nz, lax.rem(me, self.nz)

    def peers(self):
        me, x, z = self.place()
        return [
            (self.nz - 1, lambda k: {SEQ: x * self.nz + lax.rem(z + k + 1, self.nz)}),
            (self.nx - 1, lambda k: {SEQ: lax.rem(x + k + 1, self.nx) * self.nz + z}),
        ]

    def along_z(self, a, o, sems, k, received):
        me, x, z = self.place()
        at = lax.rem(z + self.nz - k, self.nz) if received else z
        return remote(
            a, o.at[x * self.nz + at], sems[0], sems[1].at[k],
            {SEQ: x * self.nz + lax.rem(z + k, self.nz)},
        )

    def along_x(self, a, o, sems, k, m):
        me, x, z = self.place()
        at = x * self.nz + lax.rem(z + self.nz - k, self.nz)
        src = a if isinstance(k, int) and k == 0 else o.at[at]
        to = lax.rem(x + m, self.nx) * self.nz + z
        remote(src, o.at[at], sems[2], sems[3].at[m], {SEQ: to}).start()

    def own(self, a, o, sems):
        return pltpu.make_async_copy(a, o.at[lax.axis_index(SEQ)], sems[4])

    def start(self, a, o, sems):
        loop(1, self.nz, lambda k: self.along_z(a, o, sems, k, False).start())
        loop(1, self.nx, lambda m: self.along_x(a, o, sems, 0, m))
        self.own(a, o, sems).start()

    def middle(self, a, o, sems):
        def forward(k):
            self.along_z(a, o, sems, k, True).wait_recv()
            loop(1, self.nx, lambda m: self.along_x(a, o, sems, k, m))

        loop(1, self.nz, forward)

    def landed(self, a, o, sems):
        self.own(a, o, sems).wait()
        loop(1, self.nx, lambda m: arrived(first_blocks(o, self.nz), sems[3].at[m]))

    def sent(self, a, o, sems):
        left(first_blocks(o, self.nz - 1), sems[0])
        left(first_blocks(o, self.nz * (self.nx - 1)), sems[2])


class GatherVar:
    def __init__(self, n, dst=slot, blocks=first_blocks):
        self.n, self.ny, self.dst, self.blocks = n, n // 2, dst, blocks

    def sems(self):
        return [dma(), dma(self.ny), dma(), dma(), dma()]

    def place(self):
        me = lax.axis_index(VAR)
        return me, me // 2, lax.rem(me, 2)

    def far(self, src, o, sems, block, way, k):
        me, y, c = self.place()
        at = 2 * lax.rem(y + self.ny - block, self.ny) + c
        src = self.dst(o, at) if src is None else src
        return remote(
            src, self.dst(o, at), sems[0], sems[1].at[k], {VAR: 2 * lax.rem(y + way, self.ny) + c}
        )

    def arrived(self, a, o, sems, k):
        me, y, c = self.place()
        arrived(self.dst(o, 2 * lax.rem(y + self.ny - k, self.ny) + c), sems[1].at[k])

    def across(self, o, sems, k, first=None):
        me, y, c = self.place()
        at = self.dst(o, 2 * lax.rem(y + self.ny - k, self.ny) + c)
        remote(at if first is None else first, at, sems[2], sems[3], {VAR: 2 * y + 1 - c}).start()

    def own(self, a, o, sems):
        return pltpu.make_async_copy(a, self.dst(o, lax.axis_index(VAR)), sems[4])

    def begin(self, a, o, sems):
        loop(1, self.ny, lambda k: self.far(a, o, sems, 0, k, k).start())

    def start(self, a, o, sems):
        self.begin(a, o, sems)
        self.across(o, sems, 0, a)
        self.own(a, o, sems).start()

    def middle(self, a, o, sems):
        def forward(k):
            self.arrived(a, o, sems, k)
            self.across(o, sems, k)

        loop(1, self.ny, forward)

    def landed(self, a, o, sems):
        self.own(a, o, sems).wait()
        arrived(self.blocks(o, self.ny), sems[3])

    def sent(self, a, o, sems):
        left(self.blocks(o, self.ny - 1), sems[0])
        left(self.blocks(o, self.ny), sems[2])


class RingVar(GatherVar):
    def begin(self, a, o, sems):
        self.far(a, o, sems, 0, 1, 1).start()
        self.far(a, o, sems, 0, self.ny - 1, self.ny - 1).start()

    def step(self, a, o, sems, t):
        half = self.ny // 2
        self.arrived(a, o, sems, t)
        if t < half:
            self.far(None, o, sems, t, 1, t + 1).start()
        self.across(o, sems, t)
        if t < half:
            self.arrived(a, o, sems, self.ny - t)
            if t < half - 1:
                self.far(None, o, sems, self.ny - t, self.ny - 1, self.ny - t - 1).start()
            self.across(o, sems, self.ny - t)


class TwoStepVar(GatherVar):
    def begin(self, a, o, sems):
        for k in (2, 6, 1, 7):
            self.far(a, o, sems, 0, k, k).start()

    def opposite(self, o, sems):
        me, y, c = self.place()
        return self.far(None, o, sems, 2 + 4 * c, 2 + 4 * c, 4)

    def middle(self, a, o, sems):
        me, y, c = self.place()
        self.arrived(a, o, sems, 2)
        self.arrived(a, o, sems, 6)
        self.opposite(o, sems).start()
        self.far(None, o, sems, 2, 1, 3).start()
        self.far(None, o, sems, 6, 7, 5).start()
        for k in (2, 6):
            self.across(o, sems, k)
        for k in (1, 7, 3, 5, 4):
            self.arrived(a, o, sems, k)
            self.across(o, sems, k)


class ReduceVar:
    def __init__(self, n):
        self.n, self.ny = n, n // 2

    def sems(self):
        return [dma(), dma(self.ny), dma(), dma()]

    def place(self):
        me = lax.axis_index(VAR)
        return me // 2, lax.rem(me, 2)

    def across(self, b, held, sems, k):
        y, c = self.place()
        yy = lax.rem(y + k + 1, self.ny)
        return remote(b.at[2 * yy + 1 - c], held.at[yy], sems[0], sems[1].at[k], {VAR: 2 * y + 1 - c})

    def along_y(self, summed, landed, sems, k):
        y, c = self.place()
        yy = lax.rem(y + k + 1, self.ny)
        remote(summed.at[yy], landed.at[y], sems[2], sems[3], {VAR: 2 * yy + c}).start()

    def start(self, b, held, summed, landed, sems):
        loop(0, self.ny, lambda k: self.across(b, held, sems, k).start())

    def push(self, b, held, summed, landed, sems):
        y, c = self.place()

        def add(k):
            yy = lax.rem(y + k + 1, self.ny)
            self.across(b, held, sems, k).wait_recv()
            total = b[2 * yy + c].astype(F32) + held[yy].astype(F32)
            summed[yy] = total.astype(summed.dtype)

        def step(k):
            add(k)
            self.along_y(summed, landed, sems, k)

        loop(0, self.ny - 1, step)
        add(self.ny - 1)

    def landed(self, b, held, summed, landed, sems):
        y, c = self.place()
        total = summed[y].astype(F32)
        arrived(first_blocks(landed, self.ny - 1), sems[3])
        for k in range(self.ny - 1):
            total = total + landed[lax.rem(y + self.ny - k - 1, self.ny)].astype(F32)
        return total

    def sent(self, b, held, summed, landed, sems):
        left(first_blocks(b, self.ny), sems[0])
        left(first_blocks(landed, self.ny - 1), sems[2])


class ReduceSeq:
    def __init__(self, n):
        self.nz, self.nx = NZ, n // NZ

    def sems(self):
        return [dma(), dma(self.nz), dma(), dma()]

    def place(self):
        me = lax.axis_index(SEQ)
        return me // self.nz, lax.rem(me, self.nz)

    def along_x(self, b, held, sems, k, m):
        x, z = self.place()
        zz = lax.rem(z + k + 1, self.nz)
        to = lax.rem(x + m, self.nx)
        remote(
            b.at[to * self.nz + zz], held.at[x * self.nz + zz], sems[0], sems[1].at[k], {SEQ: to * self.nz + z}
        ).start()

    def along_z(self, summed, landed, sems, k):
        x, z = self.place()
        zz = lax.rem(z + k + 1, self.nz)
        remote(summed.at[zz], landed.at[z], sems[2], sems[3], {SEQ: x * self.nz + zz}).start()

    def start(self, b, held, summed, landed, sems):
        def send(k):
            loop(1, self.nx, lambda m: self.along_x(b, held, sems, k, m))

        loop(0, self.nz, send)

    def push(self, b, held, summed, landed, sems):
        x, z = self.place()

        def add(k):
            zz = lax.rem(z + k + 1, self.nz)
            total = b[x * self.nz + zz].astype(F32)
            arrived(first_blocks(held, self.nx - 1), sems[1].at[k])
            for m in range(1, self.nx):
                total = total + held[lax.rem(x + self.nx - m, self.nx) * self.nz + zz].astype(F32)
            summed[zz] = total.astype(summed.dtype)

        def step(k):
            add(k)
            self.along_z(summed, landed, sems, k)

        loop(0, self.nz - 1, step)
        add(self.nz - 1)

    def landed(self, b, held, summed, landed, sems):
        x, z = self.place()
        total = summed[z].astype(F32)
        arrived(first_blocks(landed, self.nz - 1), sems[3])
        for k in range(self.nz - 1):
            total = total + landed[lax.rem(z + self.nz - k - 1, self.nz)].astype(F32)
        return total

    def sent(self, b, held, summed, landed, sems):
        left(first_blocks(b, self.nz * (self.nx - 1)), sems[0])
        left(first_blocks(landed, self.nz - 1), sems[2])


def bound(job, sems, refs):
    def fill(phase):
        return lambda *more: phase(*refs, sems, *more)

    return SimpleNamespace(
        **{name: fill(getattr(job, name)) for name in dir(job) if not name.startswith("_") and name != "n"
           and callable(getattr(job, name))}
    )


def barrier(groups):
    sem = pltpu.get_barrier_semaphore()
    for count, to in groups:
        loop(0, count, lambda k: pl.semaphore_signal(sem, inc=1, device_id=to(k), device_id_type=MESH))
    return lambda: pl.semaphore_wait(sem, sum(count for count, _ in groups))


def dot(a, b, dims=((1,), (0,))):
    return lax.dot_general(a, b, (dims, ((), ())), preferred_element_type=F32)


def over_vars(fold, z):
    out = z[:, :128]
    for at in range(128, z.shape[1], 128):
        out = fold(out, z[:, at : at + 128])
    for shift in (64, 32, 16):
        out = fold(out, pltpu.roll(out, shift, 1))
    return jnp.concatenate([out] * (z.shape[1] // 128), axis=1)


def program(n_var, n_seq, tokens, agg_query, agg_value, w_query, w_key, w_value, gain, grad_out):
    factor = HD ** (-0.5)
    per, rows, width = tokens.shape
    heads = agg_query.shape[0]
    octets = heads // 8
    cut = width // n_var
    own = rows // n_var
    line = own * heads
    groups = rows // 16
    chunk = per * 16
    lanes = n_var * chunk
    tall = 16 * heads
    row_count = n_seq * own
    at_once = 16 // own
    ny, nz, nx = n_var // 2, NZ, n_seq // NZ
    share = heads // nx

    at_cut = lambda j: pl.ds(pl.multiple_of(j * cut, cut), cut)
    few = lambda j: pl.ds(pl.multiple_of(j * share, share), share)
    weight = lambda w: RingVar(
        n_var, lambda o, j: o.at[j, :, pl.ds(w * HD, HD)], lambda o, n: o.at[pl.ds(0, n), :, pl.ds(w * HD, HD)]
    )
    jobs = dict(
        tokens=Direct(VAR, n_var, lambda x, j: x.at[:, :, at_cut(j)], slot),
        scores=GatherVar(n_var),
        value=GatherSeq(n_seq),
        pooled=ReduceVar(n_var),
        normed=GatherSeq(n_seq),
        w_query=weight(0),
        w_key=weight(1),
        w_value=weight(2),
        kv=TwoStepVar(n_var),
        dkv=ReduceVar(n_var),
        grad=ReduceSeq(n_seq),
        d_pooled=GatherVar(n_var),
        dmix=ReduceVar(n_var),
        dscore=GatherVar(n_var),
        back=Direct(VAR, n_var, slot, lambda o, j: o.at[:, at_cut(j)], lambda o, n: o.at[:, pl.ds(0, n * cut)]),
        query_z=Direct(Z, nz, whole),
        query_x=Direct(X, nx, lambda x, j: x.at[few(j)]),
        query=GatherVar(n_var, lambda o, j: o.at[:, at_cut(j)], lambda o, n: o.at[:, pl.ds(0, n * cut)]),
        query_all=Direct(X, nx, whole, lambda o, j: o.at[few(j)], lambda o, n: o.at[pl.ds(0, n * share)]),
    )

    block = lambda n, r=line, c=HD, t=BF16: ((n, r, c), t)

    def through(blocks, *rest):
        return block(blocks, *rest), block(ny, *rest), block(ny, *rest), block(ny, *rest)

    pooled, dkv = through(n_var), through(n_var, row_count, 2 * HD)
    dmix = through(n_var, 8, lanes, F32)
    buffers = dict(
        grouped=((n_var, per, rows, cut), BF16),
        s_own=((heads, (per + 1) * rows), BF16),
        s_all=block(n_var, heads, (per + 1) * rows),
        value_all=block(n_seq, cut, HD),
        mix=block(n_var, 8, lanes, F32),
        mix_wide=block(groups, tall, lanes),
        mix_tall=block(groups, lanes, tall),
        summary=block(groups, tall, cut),
        stack=block(groups, tall, HD),
        pooled0=pooled[0], pooled1=pooled[1], pooled2=pooled[2], pooled3=pooled[3],
        unit=((line, HD), F32),
        inv=((line, HD), F32),
        normed_own=((line, HD), BF16),
        normed_all=block(n_seq),
        weights=block(n_var, cut, 3 * HD),
        wide=((row_count, width), BF16),
        kv_own=((row_count, 2 * HD), BF16),
        kv_all=block(n_var, row_count, 2 * HD),
        dkv0=dkv[0], dkv1=dkv[1], dkv2=dkv[2], dkv3=dkv[3],
        grad0=block(n_seq), grad1=block(n_seq), grad2=block(nz), grad3=block(nz),
        dp_own=((line, HD), BF16),
        dp_all=block(n_var),
        d_summary=block(groups, tall, cut),
        dmix0=dmix[0], dmix1=dmix[1], dmix2=dmix[2], dmix3=dmix[3],
        dscore_own=((16, lanes // 2), BF16),
        dscore_all=block(n_var, 16, lanes // 2),
        back_b=block(n_var, per * rows, cut),
        query_part=((heads, cut), F32),
        query_line=((heads, cut), F32),
        query_done=((share, cut), F32),
        query_wide=((share, width), F32),
        query_z=block(nz, heads, cut, F32),
        query_x=block(nx, share, cut, F32),
    )
    results = dict(
        attended=((row_count, HD), BF16),
        mixed=((per * rows, width), BF16),
        through_scores=((per * rows, width), BF16),
        d_query=((heads, width), F32),
    )
    names = [*results, *buffers]
    job_sems = [job.sems() for job in jobs.values()]

    def kernel(tok, aq, av, wq, wk, wv, gn, go, *rest):
        r = SimpleNamespace(**dict(zip(names, rest)))
        refs = dict(
            tokens=(tok, r.grouped),
            scores=(r.s_own, r.s_all),
            value=(av, r.value_all),
            pooled=(r.pooled0, r.pooled1, r.pooled2, r.pooled3),
            normed=(r.normed_own, r.normed_all),
            w_query=(wq, r.weights),
            w_key=(wk, r.weights),
            w_value=(wv, r.weights),
            kv=(r.kv_own, r.kv_all),
            dkv=(r.dkv0, r.dkv1, r.dkv2, r.dkv3),
            grad=(r.grad0, r.grad1, r.grad2, r.grad3),
            d_pooled=(r.dp_own, r.dp_all),
            dmix=(r.dmix0, r.dmix1, r.dmix2, r.dmix3),
            dscore=(r.dscore_own, r.dscore_all),
            back=(r.back_b, r.mixed),
            query_z=(r.query_part, r.query_z),
            query_x=(r.query_line, r.query_x),
            query=(r.query_done, r.query_wide),
            query_all=(r.query_wide, r.d_query),
        )
        left, ready_jobs = list(rest[len(names) :]), {}
        for (name, job), wanted in zip(jobs.items(), job_sems):
            ready_jobs[name] = bound(job, left[: len(wanted)], refs[name])
            left = left[len(wanted) :]
        j = SimpleNamespace(**ready_jobs)
        ring = (j.w_key, j.w_value, j.w_query)

        def t_group(g):
            return r.grouped[:, :, g * 16 : (g + 1) * 16, :].reshape(lanes, cut)

        i = lax.axis_index(VAR)
        greeted = barrier(jobs["tokens"].peers() + jobs["value"].peers())

        local = dot(aq[...], tok[...].reshape(per * rows, width), NT) * factor
        scaled = [local[:, v * rows : (v + 1) * rows] for v in range(per)]
        top = functools.reduce(jnp.maximum, scaled).astype(BF16).astype(F32)
        r.s_own[...] = jnp.concatenate([*[jnp.exp(part - top) for part in scaled], top], axis=1).astype(BF16)
        greeted()
        j.scores.start()
        j.value.start()
        j.tokens.start()
        for w in ring:
            w.start()
        j.scores.middle()
        j.value.middle()

        iota = lambda shape, dim: lax.broadcasted_iota(jnp.int32, shape, dim)
        ones = lambda where: where.astype(F32).astype(BF16)
        wide_mask = lax.rem(iota((16, lanes), 1), 16) == iota((16, lanes), 0)
        tall_mask = lax.rem(iota((lanes, tall), 0), 16) == lax.rem(iota((lanes, tall), 1), 16)
        spread_heads = ones(iota((heads, tall), 1) // 16 == iota((heads, tall), 0))
        at, to = iota((tall, tall), 0), iota((tall, tall), 1)
        to_patches = ones(to == lax.rem(at, heads) * 16 + at // heads)
        to_heads = ones(to == lax.rem(at, 16) * heads + at // 16)

        j.scores.landed()
        scores = r.s_all[...].astype(F32)
        for g in range(groups):
            picked = lambda n, v: scores[n, :, v * rows + g * 16 : v * rows + (g + 1) * 16]
            over = lambda pick: jnp.concatenate([pick(n, v) for n in range(n_var) for v in range(per)], axis=1)
            tops = over(lambda n, v: picked(n, per))
            e = over(picked) * jnp.exp(tops - over_vars(jnp.maximum, tops))
            mixw = e / over_vars(jnp.add, e)
            for o in range(octets):
                r.mix[g * octets + o] = mixw[o * 8 : (o + 1) * 8]
            mix_b = mixw.astype(BF16)
            full = jnp.broadcast_to(mix_b.astype(F32)[:, None, :], (heads, 16, lanes))
            full = jnp.where(wide_mask[None], full, 0.0)
            r.mix_wide[g] = full.astype(BF16).reshape(tall, lanes)
            r.mix_tall[g] = jnp.where(tall_mask, dot(mix_b, spread_heads, TN), 0.0).astype(BF16)
        j.value.landed()
        j.scores.sent()
        j.value.sent()
        j.tokens.landed()

        for g in range(groups):
            r.summary[g] = dot(r.mix_wide[g], t_group(g)).astype(BF16)
        for h in range(heads):
            here = slice(h * 16, (h + 1) * 16)
            part = jnp.concatenate([r.summary[g, here, :] for g in range(groups)], axis=0)
            part = dot(part, r.value_all[h]).astype(BF16)
            for g in range(groups):
                r.stack[g, here, :] = part[g * 16 : (g + 1) * 16]
        for g in range(groups):
            part = dot(to_patches, r.stack[g]).astype(BF16)
            for n in range(at_once):
                r.pooled0[g * at_once + n] = part[n * line : (n + 1) * line]
        j.pooled.start()
        j.pooled.push()
        for w in ring:
            w.step(1)
        pooled = j.pooled.landed().astype(BF16).astype(F32).reshape(own, heads, HD)
        mean = lambda a: jnp.sum(jnp.sum(a, axis=1, keepdims=True), axis=2, keepdims=True) / width
        center = mean(pooled)
        inv_std = lax.rsqrt(mean((pooled - center) ** 2) + EPS)
        unit = (pooled - center) * inv_std
        r.normed_own[...] = (unit * gn[...][None]).astype(BF16).reshape(line, HD)
        j.normed.start()
        r.unit[...] = unit.reshape(line, HD)
        r.inv[...] = jnp.broadcast_to(inv_std, (own, heads, HD)).reshape(line, HD)
        for w in ring:
            w.step(2)
        j.normed.middle()
        for t in range(3, ny // 2 + 1):
            for w in ring:
                w.step(t)
        j.normed.landed()

        def widen(g):
            src = r.normed_all[pl.ds(g * at_once, at_once)].reshape(tall, HD)
            part = dot(to_heads, src).astype(BF16)
            for h in range(heads):
                r.wide[pl.ds(pl.multiple_of(g * 16, 16), 16), h * HD : (h + 1) * HD] = part[h * 16 : (h + 1) * 16]

        loop(0, n_seq // at_once, widen)
        j.w_key.landed()
        j.w_value.landed()
        kv_weights = r.weights[:, :, HD:].reshape(width, 2 * HD)
        r.kv_own[...] = dot(r.wide[...], kv_weights).astype(BF16)
        j.kv.start()
        j.w_query.landed()
        queries = dot(r.wide[...], r.weights[:, :, :HD].reshape(width, HD)).astype(BF16)
        j.kv.middle()
        j.kv.landed()

        keys = r.kv_all[:, :, :HD].reshape(n_var * row_count, HD)
        values = r.kv_all[:, :, HD:].reshape(n_var * row_count, HD)
        grad = go[...]
        logits = dot(queries, keys, NT) * factor
        expo = jnp.exp(logits - jnp.max(logits, axis=1, keepdims=True))
        probs = expo / jnp.sum(expo, axis=1, keepdims=True)
        probs_b = probs.astype(BF16)
        dprob = dot(grad, values, NT)
        dlogit = (probs * (dprob - jnp.sum(probs * dprob, axis=1, keepdims=True)) * factor).astype(BF16)
        r.dkv0[:, :, :HD] = dot(dlogit, queries, TN).astype(BF16).reshape(n_var, row_count, HD)
        r.dkv0[:, :, HD:] = dot(probs_b, grad, TN).astype(BF16).reshape(n_var, row_count, HD)
        j.dkv.start()
        r.attended[...] = dot(probs_b, values).astype(BF16)
        dquery = dot(dlogit, keys).astype(BF16)
        j.dkv.push()
        dkv = j.dkv.landed().astype(BF16)

        dqkv = jnp.concatenate([dquery, dkv], axis=1)
        r.wide[...] = dot(dqkv, r.weights[...].reshape(width, 3 * HD), NT).astype(BF16)

        def narrow(g):
            at = pl.ds(pl.multiple_of(g * 16, 16), 16)
            src = jnp.concatenate([r.wide[at, h * HD : (h + 1) * HD] for h in range(heads)], axis=0)
            part = dot(to_patches, src).astype(BF16)
            for n in range(at_once):
                r.grad0[g * at_once + n] = part[n * line : (n + 1) * line]

        loop(0, n_seq // at_once, narrow)
        j.grad.start()
        j.grad.push()
        scaled = j.grad.landed().reshape(own, heads, HD) * gn[...][None]
        unit = r.unit[...].reshape(own, heads, HD)
        inv_std = r.inv[...].reshape(own, heads, HD)
        d_pooled = inv_std * (scaled - mean(scaled) - unit * mean(scaled * unit))
        r.dp_own[...] = d_pooled.astype(BF16).reshape(line, HD)
        j.d_pooled.start()
        j.d_pooled.middle()
        j.d_pooled.landed()

        for g in range(groups):
            src = r.dp_all[g * at_once : (g + 1) * at_once].reshape(tall, HD)
            r.stack[g] = dot(to_heads, src).astype(BF16)
        for h in range(heads):
            here = slice(h * 16, (h + 1) * 16)
            part = jnp.concatenate([r.stack[g, here, :] for g in range(groups)], axis=0)
            part = dot(part, r.value_all[h], NT).astype(BF16)
            for g in range(groups):
                r.d_summary[g, here, :] = part[g * 16 : (g + 1) * 16]
        for g in range(groups):
            part = dot(r.mix_tall[g], r.d_summary[g]).astype(BF16).reshape(n_var, per, 16, cut)
            for v in range(per):
                r.back_b[:, v * rows + g * 16 : v * rows + (g + 1) * 16, :] = part[:, v]
        j.back.some(0, 1, 2)
        for g in range(groups):
            cross = dot(r.d_summary[g], t_group(g), NT).reshape(heads, 16, lanes)
            dmix = jnp.sum(jnp.where(wide_mask[None], cross, 0.0), axis=1)
            for o in range(octets):
                r.dmix0[g * octets + o] = dmix[o * 8 : (o + 1) * 8]
        j.dmix.start()
        j.dmix.push()
        j.back.some(3)
        dmix = j.dmix.landed()
        mixw = r.mix[i]
        dscore = mixw * (dmix - over_vars(jnp.add, mixw * dmix)) * factor
        r.dscore_own[...] = jnp.concatenate([dscore[:, : lanes // 2], dscore[:, lanes // 2 :]], axis=0).astype(BF16)
        j.dscore.start()
        j.back.some(4)
        j.dscore.middle()
        j.dscore.landed()
        j.back.some(7, 6)

        query_part = jnp.zeros((heads, cut), F32)
        mine = jnp.zeros((heads, per * rows), F32)
        lane, column = iota((lanes, per * rows), 0) - i * chunk, iota((lanes, per * rows), 1)
        for g in range(groups):
            halves = r.dscore_all[g * octets : (g + 1) * octets].astype(F32)
            dscore = jnp.concatenate([halves[:, :8], halves[:, 8:]], axis=2).reshape(heads, lanes).astype(BF16)
            query_part = query_part + dot(dscore, t_group(g))
            at_lane = column // rows * 16 + lax.rem(column, 16)
            here = (lane == at_lane) & (lax.rem(column, rows) // 16 == g)
            mine = mine + dot(dscore, ones(here))
        r.query_part[...] = query_part
        j.query_z.start()
        j.query_z.landed()
        r.query_line[...] = jnp.sum(r.query_z[...], axis=0)
        j.query_x.start()
        j.query_x.landed()
        r.query_done[...] = jnp.sum(r.query_x[...], axis=0)
        j.query.start()
        j.back.some(8, 5)
        j.query.middle()
        for job in (j.tokens, j.pooled, j.normed, *ring, j.kv, j.dkv, j.grad, j.d_pooled, j.dmix, j.dscore):
            job.sent()
        j.query.landed()
        j.query_all.start()
        r.through_scores[...] = dot(mine.astype(BF16), aq[...], TN).astype(BF16)
        j.query_z.sent()
        j.query_x.sent()
        j.query.sent()
        j.query_all.landed()
        j.query_all.sent()
        j.back.landed()
        j.back.sent()

    in_vmem = pl.BlockSpec(memory_space=pltpu.VMEM)
    return pl.pallas_call(
        kernel,
        name="encoder",
        out_shape=[jax.ShapeDtypeStruct(*results[name]) for name in results],
        in_specs=[in_vmem] * 8,
        out_specs=[in_vmem] * len(results),
        scratch_shapes=[pltpu.VMEM(*buffers[name]) for name in buffers]
        + [sem for wanted in job_sems for sem in wanted],
        compiler_params=pltpu.CompilerParams(
            collective_id=0, has_side_effects=True, vmem_limit_bytes=60 * 1024 * 1024
        ),
    )(tokens, agg_query, agg_value, w_query, w_key, w_value, gain, grad_out)


def per_device(n_var, n_seq, tokens, agg_query, agg_value, w_query, w_key, w_value, gain, d_out):
    heads = agg_query.shape[0]
    attended, mixed, through_scores, d_query = program(
        n_var, n_seq, tokens, agg_query, agg_value, w_query, w_key, w_value,
        gain.reshape(heads, HD), d_out.reshape(-1, HD),
    )
    d_tokens = (mixed.astype(F32) + through_scores.astype(F32)).astype(BF16).reshape(tokens.shape)
    return (attended.reshape(d_out.shape), d_tokens, d_query)


def solution(mesh):
    return jax.shard_map(
        functools.partial(per_device, mesh.shape[VAR], mesh.shape[SEQ]),
        mesh=mesh,
        in_specs=(
            P(VAR, SEQ, None),
            P(),
            P(VAR, SEQ),
            P(VAR, SEQ),
            P(VAR, SEQ),
            P(VAR, SEQ),
            P(),
            P(None, VAR, SEQ),
        ),
        out_specs=(P(None, VAR, SEQ), P(VAR, SEQ, None), P()),
        check_vma=False,
    )
```
